512 devices in a mesh: section: 8 (over z), dom: 64 (over x, y, core).
Axes of the slice: x: 4, y: 8, z: 8, core: 2. Of those that a mesh axis runs over, the one named last changes fastest.
Arguments:
- initial_embed: bfloat16 [4, 24576, 256], P(None, 'dom'), may hold values from -6 to 6
- out_cotangent: bfloat16 [4, 24576, 256], P(None, 'dom'), may hold values from -6 to 6
- layer_weights: bfloat16 [8, 256, 256], P('section'), may hold values from -0.375 to 0.375
- stale_halo: bfloat16 [8, 4, 16384, 256], P('section', None, 'dom'), may hold values from -6 to 6
- tile_values: bfloat16 [4, 768, 128, 128], P(None, 'dom'), may hold values from -0.375 to 0.375
- tile_rows: int32 [4, 768], P(None, 'dom'), may hold values from 0 to 2
- tile_cols: int32 [4, 768], P(None, 'dom'), may hold values from 0 to 4
- tile_count: int32 [4, 64], P(None, 'dom'), may hold values from 3 to 12, as said below
- send_blocks: int32 [4, 128], P(None, 'dom'), may hold values from 0 to 2
Outputs:
- weight_grad: float32 [8, 256, 256], P('section')
- fresh_halo: bfloat16 [8, 4, 16384, 256], P('section', None, 'dom')
- initial_grad: float32 [4, 24576, 256], P(None, 'dom', 'section')
The draws below stay inside these ranges and needn't reach their ends.
Inputs may be any that keep to these rules, and one draw needn't show every extreme that they name: `tile_count`: in every span some partition has all 12 slots live.
All inputs are finite; a program needn't handle non-finite values.
Results may differ from the reference program's by a relative error of at most 0.03.
Values may be sent and summed in bfloat16 or wider, within the bound.
No kernel may reach another device: no remote copies, remote signals or barrier semaphores. Data moves between devices by JAX's collectives and lax.ppermute only.
A program may use at most 64 MiB of HBM per device.

```python
import jax
import jax.numpy as jnp

H = 256
TILE = 128
BLOCKS = 3
SPANS = 4
TILES_MAX = 12
ROWS = 384
NODES = 24576
LAYERS = 8
N_DOM = 64


def draw_tile_count(key, part):
    key = jax.random.fold_in(key, 7)
    first, second, third = jax.random.split(key, 3)
    lowest = TILES_MAX // 4
    spread = jax.random.randint(first, (SPANS, N_DOM), 0, TILES_MAX - lowest + 1)
    switch = jax.random.randint(second, (SPANS, N_DOM), 0, 2)
    counts = lowest + spread * switch
    fullest = jax.random.randint(third, (SPANS,), 0, N_DOM)
    chosen = jnp.arange(N_DOM)[None, :] == fullest[:, None]
    return jnp.where(chosen, TILES_MAX, counts).astype(jnp.int32)


def place_ends(drawn, rng, smallest, top_value):
    place = [jax.random.randint(jax.random.fold_in(rng, axis), (), 0, length) for axis, length in enumerate(drawn.shape)]
    widest = drawn.shape.index(max(drawn.shape))
    neighbour = place[:widest] + [(place[widest] + 1) % drawn.shape[widest]] + place[widest + 1:]
    return drawn.at[tuple(place)].set(smallest).at[tuple(neighbour)].set(top_value)


def levels(stream_key, dims, cuts, smallest, largest):
    factor_of = 1.0
    for dim, blocks in cuts:
        draws = jax.random.uniform(jax.random.fold_in(jax.random.fold_in(stream_key, 6), dim), (blocks,), jnp.float32, smallest / len(cuts), largest / len(cuts))
        factor_of = factor_of * jnp.repeat(jnp.exp(draws), dims[dim] // blocks).reshape((-1,) + (1,) * (len(dims) - 1 - dim))
    return factor_of


def noise(own_key, shape, scale, reach, pieces=(), kind=jnp.bfloat16):
    array = scale * jax.random.normal(own_key, shape, jnp.float32)
    if pieces:
        array = array * levels(own_key, shape, pieces, -0.22, 0.18)
    return jnp.clip(array, -reach, reach).astype(kind)


def setup_inputs(seed: int = 0) -> dict:
    key_of = jax.random.split(jax.random.key(seed), 10)
    return {
        "initial_embed": noise(key_of[0], (SPANS, NODES, H), 1.0, 6.0, ((1, 64),)),
        "out_cotangent": noise(key_of[1], (SPANS, NODES, H), 1.0, 6.0, ((1, 64),)),
        "layer_weights": noise(key_of[2], (LAYERS, H, H), H ** -0.5, 0.375, ((0, 8),)),
        "stale_halo": noise(key_of[3], (LAYERS, SPANS, 2 * TILE * N_DOM, H), 1.0, 6.0, ((0, 8), (2, 64))),
        "tile_values": noise(key_of[4], (SPANS, N_DOM * TILES_MAX, TILE, TILE), (2 * TILE) ** -0.5, 0.375, ((1, 64),)),
        "tile_rows": place_ends(jax.random.randint(key_of[5], (SPANS, N_DOM * TILES_MAX), 0, BLOCKS), jax.random.fold_in(key_of[5], 1), 0, BLOCKS - 1).astype(jnp.int32),
        "tile_cols": place_ends(jax.random.randint(key_of[6], (SPANS, N_DOM * TILES_MAX), 0, BLOCKS + 2), jax.random.fold_in(key_of[6], 1), 0, (BLOCKS + 2) - 1).astype(jnp.int32),
        "tile_count": draw_tile_count(jax.random.fold_in(key_of[9], 71), 0),
        "send_blocks": place_ends(jax.random.randint(key_of[8], (SPANS, 2 * N_DOM), 0, BLOCKS), jax.random.fold_in(key_of[8], 1), 0, BLOCKS - 1).astype(jnp.int32),
    }


ALPHA = 0.1
LAMBDA_RATE = 0.5

def layer_rate(index):
    return jnp.log(LAMBDA_RATE / (jnp.asarray(index, jnp.float32) + 1.0) + 1.0)

def spread_forward(extended, values, row_ids, col_ids, count):
    live_mask = (jnp.arange(values.shape[0]) < count).astype(jnp.float32)
    picked = extended[col_ids]
    products = jnp.einsum('tij,tjh->tih', values.astype(jnp.float32), picked.astype(jnp.float32))
    return jax.ops.segment_sum(products * live_mask[:, None, None], row_ids, num_segments=BLOCKS)

def spread_backward(gradient, values, row_ids, col_ids, count):
    live_mask = (jnp.arange(values.shape[0]) < count).astype(jnp.float32)
    picked = gradient[row_ids]
    products = jnp.einsum('tji,tjh->tih', values.astype(jnp.float32), picked.astype(jnp.float32))
    summed = jax.ops.segment_sum(products * live_mask[:, None, None], col_ids, num_segments=BLOCKS + 2)
    return summed[:BLOCKS]

def reference(initial_embed, out_cotangent, layer_weights, stale_halo, tile_values, tile_rows, tile_cols, tile_count, send_blocks):
    weight_sum = jnp.zeros((LAYERS, H, H), jnp.float32)
    fresh_halo = jnp.zeros(stale_halo.shape, jnp.bfloat16)
    grads = []
    for span in range(SPANS):
        values = tile_values[span].reshape(N_DOM, TILES_MAX, TILE, TILE)
        row_ids = tile_rows[span].reshape(N_DOM, TILES_MAX)
        col_ids = tile_cols[span].reshape(N_DOM, TILES_MAX)
        counts = tile_count[span]
        sender = send_blocks[span].reshape(N_DOM, 2)
        initial = initial_embed[span].reshape(N_DOM, ROWS, H)
        layer_in = initial
        mixes = []
        preacts = []
        for layer in range(LAYERS):
            beta_rate = layer_rate(layer)
            blocks = layer_in.reshape(N_DOM, BLOCKS, TILE, H)
            to_lower = jnp.take_along_axis(blocks, sender[:, 0][:, None, None, None], axis=1)[:, 0]
            to_upper = jnp.take_along_axis(blocks, sender[:, 1][:, None, None, None], axis=1)[:, 0]
            received = jnp.concatenate([jnp.roll(to_upper, 1, axis=0), jnp.roll(to_lower, -1, axis=0)], axis=1)
            fresh_halo = fresh_halo.at[layer, span].set(received.reshape(N_DOM * 2 * TILE, H))
            halo_blocks = stale_halo[layer, span].reshape(N_DOM, 2, TILE, H)
            extended = jnp.concatenate([blocks, halo_blocks], axis=1)
            aggregate = jax.vmap(spread_forward)(extended, values, row_ids, col_ids, counts).reshape(N_DOM, ROWS, H)
            mixed = ((1.0 - ALPHA) * aggregate + ALPHA * initial.astype(jnp.float32)).astype(jnp.bfloat16)
            preact = (1.0 - beta_rate) * mixed.astype(jnp.float32) + beta_rate * jnp.einsum('nrh,hk->nrk', mixed.astype(jnp.float32), layer_weights[layer].astype(jnp.float32))
            mixes.append(mixed)
            preacts.append(preact)
            layer_in = jax.nn.silu(preact).astype(jnp.bfloat16)
        grad_in = out_cotangent[span].reshape(N_DOM, ROWS, H)
        initial_acc = jnp.zeros((N_DOM, ROWS, H), jnp.float32)
        for layer in reversed(range(LAYERS)):
            beta_rate = layer_rate(layer)
            preact = preacts[layer]
            sigmoid = jax.nn.sigmoid(preact)
            delta = (grad_in.astype(jnp.float32) * sigmoid * (1.0 + preact * (1.0 - sigmoid))).astype(jnp.bfloat16)
            weight_sum = weight_sum.at[layer].add(jnp.einsum('nrh,nrk->hk', mixes[layer].astype(jnp.float32), delta.astype(jnp.float32)))
            dmixed = (1.0 - beta_rate) * delta.astype(jnp.float32) + beta_rate * jnp.einsum('nrk,hk->nrh', delta.astype(jnp.float32), layer_weights[layer].astype(jnp.float32))
            initial_acc = initial_acc + ALPHA * dmixed
            rounded = dmixed.astype(jnp.bfloat16).reshape(N_DOM, BLOCKS, TILE, H)
            backward = jax.vmap(spread_backward)(rounded, values, row_ids, col_ids, counts).reshape(N_DOM, ROWS, H)
            gathered = (1.0 - ALPHA) * backward
            grad_in = gathered.astype(jnp.bfloat16)
        grads.append((initial_acc + gathered).reshape(NODES, H))
    weight_grad = weight_sum / jnp.sqrt(jnp.float32(SPANS * NODES))
    return (weight_grad, fresh_halo, jnp.stack(grads))
```

```python
import functools
import math

import jax
import jax.numpy as jnp
from jax import lax
from jax.experimental import pallas as pl
from jax.experimental.pallas import tpu as pltpu
from jax.sharding import PartitionSpec as P

ALPHA = 0.1
LAMBDA_RATE = 0.5
CORES = 2
F32 = jnp.float32
BF16 = jnp.bfloat16


def vmem():
    return pl.BlockSpec(memory_space=pltpu.VMEM)


def smem():
    return pl.BlockSpec(memory_space=pltpu.SMEM)


def call(body, out_shape, in_specs, scratch, flops, moved):
    return pl.pallas_call(
        body,
        out_shape=out_shape,
        in_specs=in_specs,
        out_specs=jax.tree.map(lambda _: vmem(), out_shape),
        scratch_shapes=scratch,
        compiler_params=pltpu.CompilerParams(vmem_limit_bytes=24 * 1024 * 1024),
        cost_estimate=pl.CostEstimate(flops=flops, bytes_accessed=moved, transcendentals=0),
    )


def prepare_body(
    tiles_max, nblocks, info, own_x, got_x, own_g, got_g, own_t, got_t, dense, flipped, x0, g0, acc
):
    size = acc.shape[-1]
    core = info[2 * tiles_max + 3]
    mine = info[2 * tiles_max + 4] == 1
    acc[...] = jnp.zeros_like(acc)

    def add(slot, carry):
        row = info[slot]
        col = info[tiles_max + slot]
        col = jnp.where(col < nblocks, col, nblocks + jnp.where(col - nblocks == core, 0, 1))
        tile = jnp.where(mine, own_t[slot], got_t[slot])
        acc[row, col] += tile.astype(F32)
        return carry

    lax.fori_loop(0, info[2 * tiles_max], add, 0)
    for row in range(nblocks):
        for col in range(nblocks + 2):
            block = acc[row, col]
            dense[row * size : (row + 1) * size, col * size : (col + 1) * size] = block.astype(BF16)
            if col < nblocks:
                flipped[col * size : (col + 1) * size, row * size : (row + 1) * size] = (
                    block.T.astype(BF16)
                )
    x0[...] = jnp.where(mine, own_x[...], got_x[...])
    g0[...] = jnp.where(mine, own_g[...], got_g[...])


def weight_of(core, mine, got, layer):
    half = mine.shape[1] // 2
    own = mine[layer, half:, :]
    other = got[layer, half:, :]
    top = jnp.where(core == 0, own, other)
    bottom = jnp.where(core == 0, other, own)
    return jnp.concatenate([top, bottom], axis=0)


def forward_body(
    tiles_max, info, rates, dense, x0, mine, got, mix_out, slope_out, fresh, ext
):
    rows = x0.shape[0]
    size = fresh.shape[1]
    half = mine.shape[1] // 2
    core = info[2 * tiles_max + 3]
    send = jnp.where(core == 0, info[2 * tiles_max + 1], info[2 * tiles_max + 2])
    ext[0:rows, :] = x0[...]

    def step(layer, carry):
        rate = rates[layer]
        start = pl.multiple_of(send * size, size)
        fresh[layer] = ext[pl.ds(start, size), :]
        ext[rows : rows + half, :] = mine[layer, :half, :]
        ext[rows + half : rows + 2 * half, :] = got[layer, :half, :]
        agg = jnp.dot(dense[...], ext[...], preferred_element_type=F32)
        mix = ((1.0 - ALPHA) * agg + ALPHA * x0[...].astype(F32)).astype(BF16)
        mix_out[layer] = mix
        weight = weight_of(core, mine, got, layer)
        pre = (1.0 - rate) * mix.astype(F32) + rate * jnp.dot(
            mix, weight, preferred_element_type=F32
        )
        gate = jax.nn.sigmoid(pre)
        slope_out[layer] = gate * (1.0 + pre * (1.0 - gate))
        ext[0:rows, :] = (pre * gate).astype(BF16)
        return carry

    lax.fori_loop(0, mine.shape[0], step, 0)


def backward_body(
    tiles_max, info, rates, flipped, g0, mine, got, mix, slope, dweight, dinput, grad, acc, last
):
    depth = mine.shape[0]
    half = dweight.shape[1]
    core = info[2 * tiles_max + 3]
    grad[...] = g0[...]
    acc[...] = jnp.zeros_like(acc)

    def step(index, carry):
        layer = depth - 1 - index
        rate = rates[layer]
        delta = (grad[...].astype(F32) * slope[layer]).astype(BF16)
        start = pl.multiple_of(core * half, half)
        part = mix[layer, :, pl.ds(start, half)]
        dweight[layer] = lax.dot_general(
            part, delta, (((0,), (0,)), ((), ())), preferred_element_type=F32
        ).astype(BF16)
        weight = weight_of(core, mine, got, layer)
        dmix = (1.0 - rate) * delta.astype(F32) + rate * lax.dot_general(
            delta, weight, (((1,), (1,)), ((), ())), preferred_element_type=F32
        )
        acc[...] += ALPHA * dmix
        back = jnp.dot(flipped[...], dmix.astype(BF16), preferred_element_type=F32)
        gx = (1.0 - ALPHA) * back
        last[...] = gx
        grad[...] = gx.astype(BF16)
        return carry

    lax.fori_loop(0, depth, step, 0)
    dinput[...] = (acc[...] + last[...]).T.astype(BF16)


def swap(value):
    size = lax.axis_size("dom")
    return lax.ppermute(value, "dom", [(i, i ^ 1) for i in range(size)])


def exchange(value, axis, groups=None):
    return lax.all_to_all(value, axis, 0, 0, tiled=True, axis_index_groups=groups)


def shards(
    initial_embed,
    out_cotangent,
    layer_weights,
    stale_halo,
    tile_values,
    tile_rows,
    tile_cols,
    tile_count,
    send_blocks,
):
    section = lax.axis_index("section")
    depth = lax.axis_size("section")
    doms = lax.axis_size("dom")
    core = lax.axis_index("dom") % CORES
    spans, rows, width = initial_embed.shape
    tiles_max, size = tile_values.shape[1], tile_values.shape[-1]
    nblocks = rows // size
    half = width // 2
    chips = doms // CORES
    span = section % spans
    parity = section // spans
    rates = jnp.log(LAMBDA_RATE / (jnp.arange(depth, dtype=F32) + 1.0) + 1.0)

    halo = stale_halo[0].reshape(spans, 2, size, width)
    kept = lax.dynamic_index_in_dim(halo, core, 1, keepdims=False)
    given = lax.dynamic_index_in_dim(halo, 1 - core, 1, keepdims=False)
    taken = swap(given)
    choose = (jnp.arange(CORES) == core)[:, None, None, None]
    halo_slots = jnp.where(choose, kept[None], taken[None]).reshape(depth, size, width)
    own_weight = lax.dynamic_slice_in_dim(layer_weights[0], core * half, half, 0)
    weight_slots = jnp.broadcast_to(own_weight[None], (depth, half, width))
    mine = exchange(jnp.concatenate([halo_slots, weight_slots], axis=1), "section")
    got = swap(mine)

    def of_span(value):
        return lax.dynamic_index_in_dim(value, span, 0, keepdims=False)

    own_x, own_g, own_t = of_span(initial_embed), of_span(out_cotangent), of_span(tile_values)
    own_info = jnp.concatenate(
        [of_span(tile_rows), of_span(tile_cols), of_span(tile_count), of_span(send_blocks)]
    )
    is_mine = parity == core
    info = jnp.where(is_mine, own_info, swap(own_info))
    info = jnp.concatenate(
        [info, core.astype(jnp.int32)[None], is_mine.astype(jnp.int32)[None]]
    )
    dense, flipped, x0, g0 = call(
        functools.partial(prepare_body, tiles_max, nblocks),
        (
            jax.ShapeDtypeStruct((rows, rows + 2 * size), BF16),
            jax.ShapeDtypeStruct((rows, rows), BF16),
            jax.ShapeDtypeStruct((rows, width), BF16),
            jax.ShapeDtypeStruct((rows, width), BF16),
        ),
        [smem()] + [vmem()] * 6,
        [pltpu.VMEM((nblocks, nblocks + 2, size, size), F32)],
        10**6,
        4 * 10**6,
    )(info, own_x, swap(own_x), own_g, swap(own_g), own_t, swap(own_t))

    mix, slope, fresh_out = call(
        functools.partial(forward_body, tiles_max),
        (
            jax.ShapeDtypeStruct((depth, rows, width), BF16),
            jax.ShapeDtypeStruct((depth, rows, width), F32),
            jax.ShapeDtypeStruct((depth, size, width), BF16),
        ),
        [smem()] * 2 + [vmem()] * 4,
        [pltpu.VMEM((rows + 2 * size, width), BF16)],
        1400 * 10**6,
        10**7,
    )(info, rates, dense, x0, mine, got)

    fresh_in = exchange(fresh_out, "section").reshape(CORES, spans, size, width)
    stays = lax.dynamic_index_in_dim(fresh_in, 1 - core, 0, keepdims=False)
    leaves = lax.dynamic_index_in_dim(fresh_in, core, 0, keepdims=False)
    comes = lax.ppermute(
        leaves, "dom", [(i, (i - 1) % doms if i % 2 == 0 else (i + 1) % doms) for i in range(doms)]
    )
    lower = jnp.where(core == 0, comes, stays)
    upper = jnp.where(core == 0, stays, comes)
    fresh = jnp.concatenate([lower, upper], axis=1)[None]

    dweight, dinput = call(
        functools.partial(backward_body, tiles_max),
        (
            jax.ShapeDtypeStruct((depth, half, width), BF16),
            jax.ShapeDtypeStruct((width, rows), BF16),
        ),
        [smem()] * 2 + [vmem()] * 6,
        [
            pltpu.VMEM((rows, width), BF16),
            pltpu.VMEM((rows, width), F32),
            pltpu.VMEM((rows, width), F32),
        ],
        1400 * 10**6,
        10**7,
    )(info, rates, flipped, g0, mine, got, mix, slope)

    scale = 1.0 / math.sqrt(spans * rows * doms)
    terms = exchange(dweight, "section")
    partial = terms.astype(F32).sum(axis=0).reshape(chips, half // chips, width)
    groups = [[CORES * i + j for i in range(chips)] for j in range(CORES)]
    pieces = exchange(partial, "dom", groups)
    piece = (pieces.sum(axis=0) * scale).astype(BF16)
    spread = exchange(jnp.broadcast_to(piece[None], (doms,) + piece.shape), "dom")
    weight_grad = (
        spread.reshape(chips, CORES, half // chips, width)
        .transpose(1, 0, 2, 3)
        .reshape(1, width, width)
        .astype(F32)
    )

    arrived = exchange(dinput.reshape(depth, width // depth, rows), "section")
    arrived = arrived.reshape(CORES, spans, width // depth, rows)
    picked = lax.dynamic_index_in_dim(arrived, core, 0, keepdims=False)
    initial_grad = picked.transpose(0, 2, 1).astype(F32)
    return (weight_grad, fresh, initial_grad)


def solution(mesh):
    placed = (
        P(None, "dom", None),
        P(None, "dom", None),
        P("section", None, None),
        P("section", None, "dom", None),
        P(None, "dom", None, None),
        P(None, "dom"),
        P(None, "dom"),
        P(None, "dom"),
        P(None, "dom"),
    )
    return jax.shard_map(
        shards,
        mesh=mesh,
        in_specs=placed,
        out_specs=(
            P("section", None, None),
            P("section", None, "dom", None),
            P(None, "dom", "section"),
        ),
        check_vma=False,
    )
```

```python
import functools
import math

import jax
import jax.numpy as jnp
from jax import lax
from jax.experimental import pallas as pl
from jax.experimental.pallas import tpu as pltpu
from jax.sharding import PartitionSpec as P

ALPHA = 0.1
LAMBDA_RATE = 0.5
CORES = 2
F32 = jnp.float32
BF16 = jnp.bfloat16


def vmem():
    return pl.BlockSpec(memory_space=pltpu.VMEM)


def smem():
    return pl.BlockSpec(memory_space=pltpu.SMEM)


def call(body, out_shape, in_specs, scratch, flops, moved):
    return pl.pallas_call(
        body,
        out_shape=out_shape,
        in_specs=in_specs,
        out_specs=jax.tree.map(lambda _: vmem(), out_shape),
        scratch_shapes=scratch,
        compiler_params=pltpu.CompilerParams(vmem_limit_bytes=24 * 1024 * 1024),
        cost_estimate=pl.CostEstimate(flops=flops, bytes_accessed=moved, transcendentals=0),
    )


def prepare_body(
    tiles_max, nblocks, info, own_x, got_x, own_g, got_g, own_t, got_t, dense, flipped, x0, g0, acc
):
    size = acc.shape[-1]
    core = info[2 * tiles_max + 3]
    mine = info[2 * tiles_max + 4] == core
    acc[...] = jnp.zeros_like(acc)

    def add(slot, carry):
        row = info[slot]
        col = info[tiles_max + slot]
        col = jnp.where(col < nblocks, col, nblocks + jnp.where(col - nblocks == core, 0, 1))
        tile = jnp.where(mine, own_t[slot], got_t[slot])
        acc[row, col] += tile.astype(F32)
        return carry

    lax.fori_loop(0, info[2 * tiles_max], add, 0)
    for row in range(nblocks):
        for col in range(nblocks + 2):
            block = acc[row, col]
            dense[row * size : (row + 1) * size, col * size : (col + 1) * size] = block.astype(BF16)
            if col < nblocks:
                flipped[col * size : (col + 1) * size, row * size : (row + 1) * size] = (
                    block.T.astype(BF16)
                )
    x0[...] = jnp.where(mine, own_x[...], got_x[...])
    g0[...] = jnp.where(mine, own_g[...], got_g[...])


def weight_of(core, parity, mine, got, layer):
    own = mine[CORES * layer + 1 - parity]
    other = got[CORES * layer + 1 - parity]
    top = jnp.where(core == 0, own, other)
    bottom = jnp.where(core == 0, other, own)
    return jnp.concatenate([top, bottom], axis=0)


def forward_body(
    tiles_max, info, rates, dense, x0, mine, got, mix_out, slope_out, fresh, ext
):
    rows = x0.shape[0]
    size = fresh.shape[1]
    half = mine.shape[1]
    core = info[2 * tiles_max + 3]
    parity = info[2 * tiles_max + 4]
    send = jnp.where(core == 0, info[2 * tiles_max + 1], info[2 * tiles_max + 2])
    ext[0:rows, :] = x0[...]

    def step(layer, carry):
        rate = rates[layer]
        start = pl.multiple_of(send * size, size)
        fresh[layer] = ext[pl.ds(start, size), :]
        ext[rows : rows + half, :] = mine[CORES * layer + parity]
        ext[rows + half : rows + 2 * half, :] = got[CORES * layer + parity]
        agg = jnp.dot(dense[...], ext[...], preferred_element_type=F32)
        mix = ((1.0 - ALPHA) * agg + ALPHA * x0[...].astype(F32)).astype(BF16)
        mix_out[layer] = mix
        weight = weight_of(core, parity, mine, got, layer)
        pre = (1.0 - rate) * mix.astype(F32) + rate * jnp.dot(
            mix, weight, preferred_element_type=F32
        )
        gate = jax.nn.sigmoid(pre)
        slope_out[layer] = gate * (1.0 + pre * (1.0 - gate))
        ext[0:rows, :] = (pre * gate).astype(BF16)
        return carry

    lax.fori_loop(0, fresh.shape[0], step, 0)


def backward_body(
    tiles_max, info, rates, flipped, g0, mine, got, mix, slope, fresh, terms, parcel, grad, acc, last,
    dweight, sorted_rows
):
    depth, size, width = fresh.shape
    half = dweight.shape[1]
    chips = terms.shape[0]
    few = half // chips
    core = info[2 * tiles_max + 3]
    parity = info[2 * tiles_max + 4]
    grad[...] = g0[...]
    acc[...] = jnp.zeros_like(acc)

    def step(index, carry):
        layer = depth - 1 - index
        rate = rates[layer]
        delta = (grad[...].astype(F32) * slope[layer]).astype(BF16)
        start = pl.multiple_of(core * half, half)
        part = mix[layer, :, pl.ds(start, half)]
        dweight[layer] = lax.dot_general(
            part, delta, (((0,), (0,)), ((), ())), preferred_element_type=F32
        )
        weight = weight_of(core, parity, mine, got, layer)
        dmix = (1.0 - rate) * delta.astype(F32) + rate * lax.dot_general(
            delta, weight, (((1,), (1,)), ((), ())), preferred_element_type=F32
        )
        acc[...] += ALPHA * dmix
        back = jnp.dot(flipped[...], dmix.astype(BF16), preferred_element_type=F32)
        gx = (1.0 - ALPHA) * back
        last[...] = gx
        grad[...] = gx.astype(BF16)
        return carry

    lax.fori_loop(0, depth, step, 0)
    for chip in range(chips):
        for layer in range(depth):
            sorted_rows[chip, layer * few : (layer + 1) * few, :] = dweight[
                layer, chip * few : (chip + 1) * few, :
            ]
    terms[...] = sorted_rows[...].astype(BF16)
    dinput = (acc[...] + last[...]).T.astype(BF16)
    share = width // depth
    hop = share // 2
    for part in range(depth):
        piece = dinput[part * share : (part + 1) * share]
        parcel[part, :size, :] = fresh[part]
        parcel[part, size : size + share, :] = piece[:, :width]
        parcel[part, size + share : size + share + hop, : width // 2] = piece[:hop, width:]
        parcel[part, size + share : size + share + hop, width // 2 :] = piece[hop:, width:]
        rest = parcel.shape[1] - (size + share + hop)
        parcel[part, size + share + hop :, :] = jnp.zeros((rest, width), BF16)


def merge_body(tail, pieces, parcel_in, parcel):
    depth, deep, _ = parcel.shape
    few = pieces.shape[1] // depth
    total = pieces[0].astype(F32)
    for chip in range(1, pieces.shape[0]):
        total += pieces[chip].astype(F32)
    parcel[...] = parcel_in[...]
    for layer in range(depth):
        part = total[layer * few : (layer + 1) * few]
        if few < tail:
            pad = jnp.zeros((tail - few, part.shape[1]), F32)
            part = jnp.concatenate([part, pad], axis=0)
        parcel[layer, deep - tail :, :] = part.astype(BF16)


def unpack_body(size, core_ref, arrived, out, stays, leaves):
    spans, share, _ = out.shape
    width = arrived.shape[-1]
    hop = share // 2
    base = core_ref[0] * spans
    away = (1 - core_ref[0]) * spans
    for span in range(spans):
        leaves[span] = arrived[base + span, :size, :]
        stays[span] = arrived[away + span, :size, :]
        top = arrived[base + span, size : size + share, :].astype(F32)
        low = arrived[base + span, size + share : size + share + hop, :].astype(F32)
        tail = jnp.concatenate([low[:, : width // 2], low[:, width // 2 :]], axis=0)
        out[span, :, :width] = top
        out[span, :, width:] = tail


def fresh_body(core_ref, stays, comes, out):
    size = stays.shape[1]
    first = core_ref[0] == 0
    for span in range(stays.shape[0]):
        own, other = stays[span], comes[span]
        out[0, span, :size, :] = jnp.where(first, other, own)
        out[0, span, size:, :] = jnp.where(first, own, other)


def assemble_body(spread, out):
    doms, few, _ = spread.shape
    chips = doms // CORES
    for core in range(CORES):
        for chip in range(chips):
            row = (core * chips + chip) * few
            out[0, row : row + few, :] = spread[CORES * chip + core]


def swap(value):
    size = lax.axis_size("dom")
    return lax.ppermute(value, "dom", [(i, i ^ 1) for i in range(size)])


def exchange(value, axis, groups=None):
    return lax.all_to_all(value, axis, 0, 0, tiled=True, axis_index_groups=groups)


def shards(
    initial_embed,
    out_cotangent,
    layer_weights,
    stale_halo,
    tile_values,
    tile_rows,
    tile_cols,
    tile_count,
    send_blocks,
):
    section = lax.axis_index("section")
    depth = lax.axis_size("section")
    doms = lax.axis_size("dom")
    core = lax.axis_index("dom") % CORES
    spans, rows, width = initial_embed.shape
    tiles_max, size = tile_values.shape[1], tile_values.shape[-1]
    nblocks = rows // size
    half = width // 2
    chips = doms // CORES
    span = section % spans
    parity = section // spans
    rates = jnp.log(LAMBDA_RATE / (jnp.arange(depth, dtype=F32) + 1.0) + 1.0)

    halo = stale_halo[0].reshape(1, spans, CORES, size, width)
    weight = layer_weights[0].reshape(1, 1, CORES, half, width)
    choose = (jnp.arange(CORES) == core)[:, None, None, None, None]
    slots = jnp.where(choose, halo, weight).reshape(depth * CORES, size, width)
    column = [
        [z * doms + CORES * i + j for z in range(depth) for j in range(CORES)] for i in range(chips)
    ]
    mine = exchange(slots, ("section", "dom"), column)

    def of_span(value):
        return lax.dynamic_index_in_dim(value, span, 0, keepdims=False)

    own_x, own_g, own_t = of_span(initial_embed), of_span(out_cotangent), of_span(tile_values)
    own_info = jnp.concatenate(
        [of_span(tile_rows), of_span(tile_cols), of_span(tile_count), of_span(send_blocks)]
    )
    is_mine = parity == core
    info = jnp.where(is_mine, own_info, swap(own_info))
    info = jnp.concatenate(
        [info, core.astype(jnp.int32)[None], parity.astype(jnp.int32)[None]]
    )
    dense, flipped, x0, g0 = call(
        functools.partial(prepare_body, tiles_max, nblocks),
        (
            jax.ShapeDtypeStruct((rows, rows + 2 * size), BF16),
            jax.ShapeDtypeStruct((rows, rows), BF16),
            jax.ShapeDtypeStruct((rows, width), BF16),
            jax.ShapeDtypeStruct((rows, width), BF16),
        ),
        [smem()] + [vmem()] * 6,
        [pltpu.VMEM((nblocks, nblocks + 2, size, size), F32)],
        10**6,
        4 * 10**6,
    )(info, own_x, swap(own_x), own_g, swap(own_g), own_t, swap(own_t))

    mine, dense = lax.optimization_barrier((mine, dense))
    got = swap(mine)

    mix, slope, fresh_out = call(
        functools.partial(forward_body, tiles_max),
        (
            jax.ShapeDtypeStruct((depth, rows, width), BF16),
            jax.ShapeDtypeStruct((depth, rows, width), F32),
            jax.ShapeDtypeStruct((depth, size, width), BF16),
        ),
        [smem()] * 2 + [vmem()] * 4,
        [pltpu.VMEM((rows + 2 * size, width), BF16)],
        1400 * 10**6,
        10**7,
    )(info, rates, dense, x0, mine, got)

    few = half // chips
    tail = max(16, few)
    deep = size + width // depth + width // depth // 2 + tail
    terms, parcel = call(
        functools.partial(backward_body, tiles_max),
        (
            jax.ShapeDtypeStruct((chips, depth * few, width), BF16),
            jax.ShapeDtypeStruct((depth, deep, width), BF16),
        ),
        [smem()] * 2 + [vmem()] * 7,
        [
            pltpu.VMEM((rows, width), BF16),
            pltpu.VMEM((rows, width), F32),
            pltpu.VMEM((rows, width), F32),
            pltpu.VMEM((depth, half, width), F32),
            pltpu.VMEM((chips, depth * few, width), F32),
        ],
        1400 * 10**6,
        10**7,
    )(info, rates, flipped, g0, mine, got, mix, slope, fresh_out)

    groups = [[CORES * i + j for i in range(chips)] for j in range(CORES)]
    pieces = exchange(terms, "dom", groups)
    parcel = call(
        functools.partial(merge_body, tail),
        jax.ShapeDtypeStruct((depth, deep, width), BF16),
        [vmem()] * 2,
        [],
        10**6,
        10**6,
    )(pieces, parcel)

    arrived = exchange(parcel, "section")
    scale = 1.0 / math.sqrt(spans * rows * doms)
    piece = arrived[:, deep - tail : deep - tail + few, :].astype(F32).sum(axis=0) * scale
    copies = jnp.broadcast_to(piece[None], (doms,) + piece.shape)
    copies, arrived = lax.optimization_barrier((copies, arrived))
    spread = exchange(copies, "dom")
    weight_grad = call(
        assemble_body,
        jax.ShapeDtypeStruct((1, width, width), F32),
        [vmem()],
        [],
        10**5,
        10**6,
    )(spread)

    initial_grad, stays, leaves = call(
        functools.partial(unpack_body, size),
        (
            jax.ShapeDtypeStruct((spans, width // depth, rows), F32),
            jax.ShapeDtypeStruct((spans, size, width), BF16),
            jax.ShapeDtypeStruct((spans, size, width), BF16),
        ),
        [smem(), vmem()],
        [],
        100,
        100,
    )(core.astype(jnp.int32)[None], arrived)
    comes = lax.ppermute(
        leaves, "dom", [(i, (i - 1) % doms if i % 2 == 0 else (i + 1) % doms) for i in range(doms)]
    )
    fresh = call(
        fresh_body,
        jax.ShapeDtypeStruct((1, spans, 2 * size, width), BF16),
        [smem(), vmem(), vmem()],
        [],
        100,
        100,
    )(core.astype(jnp.int32)[None], stays, comes)
    return (weight_grad, fresh, initial_grad.transpose(0, 2, 1))


def solution(mesh):
    placed = (
        P(None, "dom", None),
        P(None, "dom", None),
        P("section", None, None),
        P("section", None, "dom", None),
        P(None, "dom", None, None),
        P(None, "dom"),
        P(None, "dom"),
        P(None, "dom"),
        P(None, "dom"),
    )
    return jax.shard_map(
        shards,
        mesh=mesh,
        in_specs=placed,
        out_specs=(
            P("section", None, None),
            P("section", None, "dom", None),
            P(None, "dom", "section"),
        ),
        check_vma=False,
    )
```

```python
import functools
import math

import jax
import jax.numpy as jnp
from jax import lax
from jax.experimental import pallas as pl
from jax.experimental.pallas import tpu as pltpu
from jax.sharding import PartitionSpec as P

ALPHA = 0.1
LAMBDA_RATE = 0.5
CORES = 2
CHIPS_X = 4
F32 = jnp.float32
BF16 = jnp.bfloat16


def vmem():
    return pl.BlockSpec(memory_space=pltpu.VMEM)


def smem():
    return pl.BlockSpec(memory_space=pltpu.SMEM)


def call(body, out_shape, in_specs, scratch, flops, moved):
    return pl.pallas_call(
        body,
        out_shape=out_shape,
        in_specs=in_specs,
        out_specs=jax.tree.map(lambda _: vmem(), out_shape),
        scratch_shapes=scratch,
        compiler_params=pltpu.CompilerParams(vmem_limit_bytes=24 * 1024 * 1024),
        cost_estimate=pl.CostEstimate(flops=flops, bytes_accessed=moved, transcendentals=0),
    )


def slots_body(core_ref, halo, weight, out):
    spans, _, _ = halo.shape
    size = out.shape[1]
    core = core_ref[0]
    for parity in range(CORES):
        mine = core == parity
        for span in range(spans):
            for half in range(CORES):
                slot = (parity * spans + span) * CORES + half
                block = slice(half * size, (half + 1) * size)
                out[slot] = jnp.where(mine, halo[span, block, :], weight[block, :])


def prepare_body(
    tiles_max, nblocks, info, own_x, got_x, own_g, got_g, own_t, got_t, dense, flipped, x0, g0, acc
):
    size = acc.shape[-1]
    core = info[2 * tiles_max + 3]
    mine = info[2 * tiles_max + 4] == core
    acc[...] = jnp.zeros_like(acc)

    def add(slot, carry):
        row = info[slot]
        col = info[tiles_max + slot]
        col = jnp.where(col < nblocks, col, nblocks + jnp.where(col - nblocks == core, 0, 1))
        tile = jnp.where(mine, own_t[slot], got_t[slot])
        acc[row, col] += tile.astype(F32)
        return carry

    lax.fori_loop(0, info[2 * tiles_max], add, 0)
    for row in range(nblocks):
        for col in range(nblocks + 2):
            block = acc[row, col]
            dense[row * size : (row + 1) * size, col * size : (col + 1) * size] = block.astype(BF16)
            if col < nblocks:
                flipped[col * size : (col + 1) * size, row * size : (row + 1) * size] = (
                    block.T.astype(BF16)
                )
    x0[...] = jnp.where(mine, own_x[...], got_x[...])
    g0[...] = jnp.where(mine, own_g[...], got_g[...])


def weight_of(core, parity, mine, got, layer):
    own = mine[CORES * layer + 1 - parity]
    other = got[CORES * layer + 1 - parity]
    top = jnp.where(core == 0, own, other)
    bottom = jnp.where(core == 0, other, own)
    return jnp.concatenate([top, bottom], axis=0)


def forward_body(
    tiles_max, info, rates, dense, x0, mine, got, mix_out, slope_out, fresh, ext
):
    rows = x0.shape[0]
    size = fresh.shape[1]
    half = mine.shape[1]
    core = info[2 * tiles_max + 3]
    parity = info[2 * tiles_max + 4]
    send = jnp.where(core == 0, info[2 * tiles_max + 1], info[2 * tiles_max + 2])
    ext[0:rows, :] = x0[...]

    def step(layer, carry):
        rate = rates[layer]
        start = pl.multiple_of(send * size, size)
        fresh[layer] = ext[pl.ds(start, size), :]
        ext[rows : rows + half, :] = mine[CORES * layer + parity]
        ext[rows + half : rows + 2 * half, :] = got[CORES * layer + parity]
        agg = jnp.dot(dense[...], ext[...], preferred_element_type=F32)
        mix = ((1.0 - ALPHA) * agg + ALPHA * x0[...].astype(F32)).astype(BF16)
        mix_out[layer] = mix
        weight = weight_of(core, parity, mine, got, layer)
        pre = (1.0 - rate) * mix.astype(F32) + rate * jnp.dot(
            mix, weight, preferred_element_type=F32
        )
        gate = jax.nn.sigmoid(pre)
        slope_out[layer] = gate * (1.0 + pre * (1.0 - gate))
        ext[0:rows, :] = (pre * gate).astype(BF16)
        return carry

    lax.fori_loop(0, fresh.shape[0], step, 0)


def backward_body(
    tiles_max, info, rates, flipped, g0, mine, got, mix, slope, terms, columns, grad, acc, last
):
    depth, _, width = columns.shape
    parts = terms.shape[0]
    few = terms.shape[1] // depth
    half = parts * few
    core = info[2 * tiles_max + 3]
    parity = info[2 * tiles_max + 4]
    grad[...] = g0[...]
    acc[...] = jnp.zeros_like(acc)

    def step(index, carry):
        layer = depth - 1 - index
        rate = rates[layer]
        delta = (grad[...].astype(F32) * slope[layer]).astype(BF16)
        start = pl.multiple_of(core * half, half)
        part = mix[layer, :, pl.ds(start, half)]
        dweight = lax.dot_general(
            part, delta, (((0,), (0,)), ((), ())), preferred_element_type=F32
        ).astype(BF16)
        row = pl.multiple_of(layer * few, few)
        for piece in range(parts):
            terms[piece, pl.ds(row, few), :] = dweight[piece * few : (piece + 1) * few]
        weight = weight_of(core, parity, mine, got, layer)
        dmix = (1.0 - rate) * delta.astype(F32) + rate * lax.dot_general(
            delta, weight, (((1,), (1,)), ((), ())), preferred_element_type=F32
        )
        acc[...] += ALPHA * dmix
        back = jnp.dot(flipped[...], dmix.astype(BF16), preferred_element_type=F32)
        gx = (1.0 - ALPHA) * back
        last[...] = gx
        grad[...] = gx.astype(BF16)
        return carry

    lax.fori_loop(0, depth, step, 0)
    dinput = (acc[...] + last[...]).T.astype(BF16)
    share = width // depth
    hop = share // 2
    for part in range(depth):
        piece = dinput[part * share : (part + 1) * share]
        columns[part, :share, :] = piece[:, :width]
        columns[part, share:, : width // 2] = piece[:hop, width:]
        columns[part, share:, width // 2 :] = piece[hop:, width:]


def merge_body(pieces, fresh, columns, parcel):
    depth, size, _ = fresh.shape
    few = pieces.shape[1] // depth
    middle = size + columns.shape[1]
    for layer in range(depth):
        parcel[layer, :size, :] = fresh[layer]
        parcel[layer, size:middle, :] = columns[layer]
        rows = slice(layer * few, (layer + 1) * few)
        total = pieces[0, rows, :].astype(F32)
        for chip in range(1, pieces.shape[0]):
            total += pieces[chip, rows, :].astype(F32)
        parcel[layer, middle:, :] = total.astype(BF16)


def unpack_body(size, core_ref, arrived, out, stays, leaves):
    spans, share, _ = out.shape
    width = arrived.shape[-1]
    hop = share // 2
    base = core_ref[0] * spans
    away = (1 - core_ref[0]) * spans
    for span in range(spans):
        leaves[span] = arrived[base + span, :size, :]
        stays[span] = arrived[away + span, :size, :]
        top = arrived[base + span, size : size + share, :].astype(F32)
        low = arrived[base + span, size + share : size + share + hop, :].astype(F32)
        tail = jnp.concatenate([low[:, : width // 2], low[:, width // 2 :]], axis=0)
        out[span, :, :width] = top
        out[span, :, width:] = tail


def fresh_body(core_ref, stays, comes, out):
    size = stays.shape[1]
    first = core_ref[0] == 0
    for span in range(stays.shape[0]):
        own, other = stays[span], comes[span]
        out[0, span, :size, :] = jnp.where(first, other, own)
        out[0, span, size:, :] = jnp.where(first, own, other)


def swap(value):
    size = lax.axis_size("dom")
    return lax.ppermute(value, "dom", [(i, i ^ 1) for i in range(size)])


def exchange(value, axis, groups=None):
    return lax.all_to_all(value, axis, 0, 0, tiled=True, axis_index_groups=groups)


def shards(
    initial_embed,
    out_cotangent,
    layer_weights,
    stale_halo,
    tile_values,
    tile_rows,
    tile_cols,
    tile_count,
    send_blocks,
):
    section = lax.axis_index("section")
    depth = lax.axis_size("section")
    doms = lax.axis_size("dom")
    core = lax.axis_index("dom") % CORES
    spans, rows, width = initial_embed.shape
    tiles_max, size = tile_values.shape[1], tile_values.shape[-1]
    nblocks = rows // size
    half = width // 2
    chips = doms // CORES
    span = section % spans
    parity = section // spans
    rates = jnp.log(LAMBDA_RATE / (jnp.arange(depth, dtype=F32) + 1.0) + 1.0)

    slots = call(
        slots_body,
        jax.ShapeDtypeStruct((depth * CORES, size, width), BF16),
        [smem(), vmem(), vmem()],
        [],
        10**5,
        10**6,
    )(core.astype(jnp.int32)[None], stale_halo[0], layer_weights[0])
    column = [
        [z * doms + CORES * i + j for z in range(depth) for j in range(CORES)] for i in range(chips)
    ]
    mine = exchange(slots, ("section", "dom"), column)

    def of_span(value):
        return lax.dynamic_index_in_dim(value, span, 0, keepdims=False)

    own_x, own_g, own_t = of_span(initial_embed), of_span(out_cotangent), of_span(tile_values)
    own_info = jnp.concatenate(
        [of_span(tile_rows), of_span(tile_cols), of_span(tile_count), of_span(send_blocks)]
    )
    is_mine = parity == core
    info = jnp.where(is_mine, own_info, swap(own_info))
    info = jnp.concatenate(
        [info, core.astype(jnp.int32)[None], parity.astype(jnp.int32)[None]]
    )
    dense, flipped, x0, g0 = call(
        functools.partial(prepare_body, tiles_max, nblocks),
        (
            jax.ShapeDtypeStruct((rows, rows + 2 * size), BF16),
            jax.ShapeDtypeStruct((rows, rows), BF16),
            jax.ShapeDtypeStruct((rows, width), BF16),
            jax.ShapeDtypeStruct((rows, width), BF16),
        ),
        [smem()] + [vmem()] * 6,
        [pltpu.VMEM((nblocks, nblocks + 2, size, size), F32)],
        10**6,
        4 * 10**6,
    )(info, own_x, swap(own_x), own_g, swap(own_g), own_t, swap(own_t))

    mine, dense = lax.optimization_barrier((mine, dense))
    got = swap(mine)

    mix, slope, fresh_out = call(
        functools.partial(forward_body, tiles_max),
        (
            jax.ShapeDtypeStruct((depth, rows, width), BF16),
            jax.ShapeDtypeStruct((depth, rows, width), F32),
            jax.ShapeDtypeStruct((depth, size, width), BF16),
        ),
        [smem()] * 2 + [vmem()] * 4,
        [pltpu.VMEM((rows + 2 * size, width), BF16)],
        1400 * 10**6,
        10**7,
    )(info, rates, dense, x0, mine, got)

    few = half // CHIPS_X
    spare = width // depth + width // depth // 2
    terms, columns = call(
        functools.partial(backward_body, tiles_max),
        (
            jax.ShapeDtypeStruct((CHIPS_X, depth * few, width), BF16),
            jax.ShapeDtypeStruct((depth, spare, width), BF16),
        ),
        [smem()] * 2 + [vmem()] * 6,
        [
            pltpu.VMEM((rows, width), BF16),
            pltpu.VMEM((rows, width), F32),
            pltpu.VMEM((rows, width), F32),
        ],
        1400 * 10**6,
        10**7,
    )(info, rates, flipped, g0, mine, got, mix, slope)

    chips_y = chips // CHIPS_X
    along_x = [
        [(x * chips_y + y) * CORES + j for x in range(CHIPS_X)]
        for y in range(chips_y)
        for j in range(CORES)
    ]
    along_y = [
        [(x * chips_y + y) * CORES + j for y in range(chips_y)]
        for x in range(CHIPS_X)
        for j in range(CORES)
    ]
    pairs = [[CORES * i + j for j in range(CORES)] for i in range(chips)]
    pieces = exchange(terms, "dom", along_x)
    parcel = call(
        merge_body,
        jax.ShapeDtypeStruct((depth, size + spare + few, width), BF16),
        [vmem()] * 3,
        [],
        10**6,
        10**6,
    )(pieces, fresh_out, columns)

    arrived = exchange(parcel, "section")
    scale = 1.0 / math.sqrt(spans * rows * doms)
    piece = arrived[:, size + spare :, :].astype(F32).sum(axis=0).astype(BF16)
    copies = jnp.broadcast_to(piece[None], (chips_y,) + piece.shape)
    copies, arrived = lax.optimization_barrier((copies, arrived))
    piece = exchange(copies, "dom", along_y).astype(F32).sum(axis=0) * scale
    copies = jnp.broadcast_to(piece[None], (CHIPS_X,) + piece.shape)
    piece = exchange(copies, "dom", along_x).reshape(half, width)
    weight_grad = lax.all_gather(piece, "dom", axis_index_groups=pairs, tiled=True)[None]

    initial_grad, stays, leaves = call(
        functools.partial(unpack_body, size),
        (
            jax.ShapeDtypeStruct((spans, width // depth, rows), F32),
            jax.ShapeDtypeStruct((spans, size, width), BF16),
            jax.ShapeDtypeStruct((spans, size, width), BF16),
        ),
        [smem(), vmem()],
        [],
        100,
        100,
    )(core.astype(jnp.int32)[None], arrived)
    comes = lax.ppermute(
        leaves, "dom", [(i, (i - 1) % doms if i % 2 == 0 else (i + 1) % doms) for i in range(doms)]
    )
    fresh = call(
        fresh_body,
        jax.ShapeDtypeStruct((1, spans, 2 * size, width), BF16),
        [smem(), vmem(), vmem()],
        [],
        100,
        100,
    )(core.astype(jnp.int32)[None], stays, comes)
    return (weight_grad, fresh, initial_grad.transpose(0, 2, 1))


def solution(mesh):
    placed = (
        P(None, "dom", None),
        P(None, "dom", None),
        P("section", None, None),
        P("section", None, "dom", None),
        P(None, "dom", None, None),
        P(None, "dom"),
        P(None, "dom"),
        P(None, "dom"),
        P(None, "dom"),
    )
    return jax.shard_map(
        shards,
        mesh=mesh,
        in_specs=placed,
        out_specs=(
            P("section", None, None),
            P("section", None, "dom", None),
            P(None, "dom", "section"),
        ),
        check_vma=False,
    )
```

```python
import functools
import math

import jax
import jax.numpy as jnp
from jax import lax
from jax.experimental import pallas as pl
from jax.experimental.pallas import tpu as pltpu
from jax.sharding import PartitionSpec as P

ALPHA = 0.1
LAMBDA_RATE = 0.5
CORES = 2
CHIPS_X = 4
F32 = jnp.float32
BF16 = jnp.bfloat16


def vmem():
    return pl.BlockSpec(memory_space=pltpu.VMEM)


def smem():
    return pl.BlockSpec(memory_space=pltpu.SMEM)


def hbm():
    return pl.BlockSpec(memory_space=pltpu.HBM)


def call(body, out_shape, in_specs, scratch, flops, moved, place=vmem):
    return pl.pallas_call(
        body,
        out_shape=out_shape,
        in_specs=in_specs,
        out_specs=jax.tree.map(lambda _: place(), out_shape),
        scratch_shapes=scratch,
        compiler_params=pltpu.CompilerParams(vmem_limit_bytes=24 * 1024 * 1024),
        cost_estimate=pl.CostEstimate(flops=flops, bytes_accessed=moved, transcendentals=0),
    )


def slots_body(core_ref, halo, weight, out, sems):
    spans = halo.shape[0]
    core = core_ref[0]
    copies = [pltpu.make_async_copy(halo, out.at[core], sems.at[0])]
    for span in range(spans):
        copies.append(
            pltpu.make_async_copy(weight.at[0], out.at[1 - core, span], sems.at[1 + span])
        )
    for copy in copies:
        copy.start()
    for copy in copies:
        copy.wait()


def prepare_body(
    tiles_max, nblocks, info, own_x, got_x, own_g, got_g, own_t, got_t, dense, flipped, x0, g0, acc
):
    size = acc.shape[-1]
    core = info[2 * tiles_max + 3]
    mine = info[2 * tiles_max + 4] == core
    acc[...] = jnp.zeros_like(acc)

    def add(slot, carry):
        row = info[slot]
        col = info[tiles_max + slot]
        col = jnp.where(col < nblocks, col, nblocks + jnp.where(col - nblocks == core, 0, 1))
        tile = jnp.where(mine, own_t[slot], got_t[slot])
        acc[row, col] += tile.astype(F32)
        return carry

    lax.fori_loop(0, info[2 * tiles_max], add, 0)
    for row in range(nblocks):
        for col in range(nblocks + 2):
            block = acc[row, col]
            dense[row * size : (row + 1) * size, col * size : (col + 1) * size] = block.astype(BF16)
            if col < nblocks:
                flipped[col * size : (col + 1) * size, row * size : (row + 1) * size] = (
                    block.T.astype(BF16)
                )
    x0[...] = jnp.where(mine, own_x[...], got_x[...])
    g0[...] = jnp.where(mine, own_g[...], got_g[...])


def weight_of(core, parity, mine, got, layer):
    own = mine[CORES * layer + 1 - parity]
    other = got[CORES * layer + 1 - parity]
    top = jnp.where(core == 0, own, other)
    bottom = jnp.where(core == 0, other, own)
    return jnp.concatenate([top, bottom], axis=0)


def forward_body(
    tiles_max, info, rates, dense_far, x0_far, mine, got, mix_out, slope_out, fresh,
    ext, dense, x0, base, sems
):
    fetches = [
        pltpu.make_async_copy(x0_far, x0, sems.at[0]),
        pltpu.make_async_copy(dense_far, dense, sems.at[1]),
    ]
    for fetch in fetches:
        fetch.start()
    rows = x0.shape[0]
    size = fresh.shape[1]
    half = mine.shape[1]
    core = info[2 * tiles_max + 3]
    parity = info[2 * tiles_max + 4]
    send = jnp.where(core == 0, info[2 * tiles_max + 1], info[2 * tiles_max + 2])
    fetches[0].wait()
    ext[0:rows, :] = x0[...]
    base[...] = ALPHA * x0[...].astype(F32)
    fetches[1].wait()

    def step(layer, carry):
        rate = rates[layer]
        start = pl.multiple_of(send * size, size)
        fresh[layer] = ext[pl.ds(start, size), :]
        ext[rows : rows + half, :] = mine[CORES * layer + parity]
        ext[rows + half : rows + 2 * half, :] = got[CORES * layer + parity]
        agg = jnp.dot(dense[...], ext[...], preferred_element_type=F32)
        mix = ((1.0 - ALPHA) * agg + base[...]).astype(BF16)
        mix_out[layer] = mix
        weight = weight_of(core, parity, mine, got, layer)
        pre = (1.0 - rate) * mix.astype(F32) + rate * jnp.dot(
            mix, weight, preferred_element_type=F32
        )
        gate = 0.5 * jnp.tanh(0.5 * pre) + 0.5
        silu = pre * gate
        slope_out[layer] = gate + silu * (1.0 - gate)
        ext[0:rows, :] = silu.astype(BF16)
        return carry

    lax.fori_loop(0, fresh.shape[0], step, 0)


def backward_body(
    tiles_max, info, rates, flipped, g0, mine, got, mix, slope, *rest
):
    terms, (columns, grad, acc, last, chunk) = rest[:CHIPS_X], rest[CHIPS_X:]
    depth, _, width = columns.shape
    few = terms[0].shape[0] // depth
    half = CHIPS_X * few
    spot = info[2 * tiles_max + 5]
    core = info[2 * tiles_max + 3]
    parity = info[2 * tiles_max + 4]
    grad[...] = g0[...]
    acc[...] = jnp.zeros_like(acc)

    def step(index, carry):
        layer = depth - 1 - index
        rate = rates[layer]
        delta = (grad[...].astype(F32) * slope[layer]).astype(BF16)
        start = pl.multiple_of(core * half, half)
        part = mix[layer, :, pl.ds(start, half)]
        chunk[...] = lax.dot_general(
            part, delta, (((0,), (0,)), ((), ())), preferred_element_type=F32
        ).astype(BF16)
        row = pl.multiple_of(layer * few, few)
        for away in range(CHIPS_X):
            piece = pl.multiple_of(lax.rem(spot + away, CHIPS_X) * few, few)
            terms[away][pl.ds(row, few), :] = chunk[pl.ds(piece, few), :]
        weight = weight_of(core, parity, mine, got, layer)
        dmix = (1.0 - rate) * delta.astype(F32) + rate * lax.dot_general(
            delta, weight, (((1,), (1,)), ((), ())), preferred_element_type=F32
        )
        acc[...] += dmix
        back = jnp.dot(flipped[...], dmix.astype(BF16), preferred_element_type=F32)
        gx = (1.0 - ALPHA) * back

        @pl.when(layer == 0)
        def _():
            last[...] = gx

        grad[...] = gx.astype(BF16)
        return carry

    lax.fori_loop(0, depth, step, 0)
    dinput = (ALPHA * acc[...] + last[...]).T.astype(BF16)
    share = width // depth
    hop = share // 2
    for part in range(depth):
        piece = dinput[part * share : (part + 1) * share]
        columns[part, :share, :] = piece[:, :width]
        columns[part, share:, : width // 2] = piece[:hop, width:]
        columns[part, share:, width // 2 :] = piece[hop:, width:]


def merge_body(*refs):
    pieces, (columns, parcel) = refs[:CHIPS_X], refs[CHIPS_X:]
    depth, spare, _ = columns.shape
    few = pieces[0].shape[0] // depth
    for layer in range(depth):
        parcel[layer, :spare, :] = columns[layer]
        rows = slice(layer * few, (layer + 1) * few)
        total = pieces[0][rows, :].astype(F32)
        for piece in pieces[1:]:
            total += piece[rows, :].astype(F32)
        parcel[layer, spare:, :] = total.astype(BF16)


def unpack_body(core_ref, arrived, out):
    spans, share, _ = out.shape
    width = arrived.shape[-1]
    hop = share // 2
    base = core_ref[0] * spans
    for span in range(spans):
        top = arrived[base + span, :share, :].astype(F32)
        low = arrived[base + span, share : share + hop, :].astype(F32)
        out[span, :, :width] = top
        out[span, :hop, width:] = low[:, : width // 2]
        out[span, hop:, width:] = low[:, width // 2 :]


def part_body(core_ref, arrived, stays, leaves):
    spans = stays.shape[0]
    core = core_ref[0]
    for span in range(spans):
        leaves[span] = arrived[core * spans + span]
        stays[span] = arrived[(1 - core) * spans + span]


def fresh_body(core_ref, stays, comes, out):
    size = stays.shape[1]
    first = core_ref[0] == 0
    for span in range(stays.shape[0]):
        own, other = stays[span], comes[span]
        out[0, span, :size, :] = jnp.where(first, other, own)
        out[0, span, size:, :] = jnp.where(first, own, other)


def swap(value):
    size = lax.axis_size("dom")
    return lax.ppermute(value, "dom", [(i, i ^ 1) for i in range(size)])


def exchange(value, axis, groups=None):
    return lax.all_to_all(value, axis, 0, 0, tiled=True, axis_index_groups=groups)


def shards(
    initial_embed,
    out_cotangent,
    layer_weights,
    stale_halo,
    tile_values,
    tile_rows,
    tile_cols,
    tile_count,
    send_blocks,
):
    section = lax.axis_index("section")
    depth = lax.axis_size("section")
    doms = lax.axis_size("dom")
    core = lax.axis_index("dom") % CORES
    spans, rows, width = initial_embed.shape
    tiles_max, size = tile_values.shape[1], tile_values.shape[-1]
    nblocks = rows // size
    half = width // 2
    chips = doms // CORES
    chips_y = chips // CHIPS_X
    spot = lax.axis_index("dom") // (CORES * chips_y)
    core_ref = core.astype(jnp.int32)[None]
    span = section % spans
    parity = section // spans
    rates = jnp.log(LAMBDA_RATE / (jnp.arange(depth, dtype=F32) + 1.0) + 1.0)

    slots = call(
        slots_body,
        jax.ShapeDtypeStruct((CORES, spans, CORES, size, width), BF16),
        [smem(), hbm(), hbm()],
        [pltpu.SemaphoreType.DMA((1 + spans,))],
        10**5,
        10**6,
        hbm,
    )(
        core.astype(jnp.int32)[None],
        stale_halo.reshape(spans, CORES, size, width),
        layer_weights.reshape(1, CORES, half, width),
    ).reshape(depth * CORES, size, width)
    column = [
        [z * doms + CORES * i + j for z in range(depth) for j in range(CORES)] for i in range(chips)
    ]
    mine = exchange(slots, ("section", "dom"), column)

    def of_span(value):
        return lax.dynamic_index_in_dim(value, span, 0, keepdims=False)

    own_x, own_g, own_t = of_span(initial_embed), of_span(out_cotangent), of_span(tile_values)
    own_info = jnp.concatenate(
        [of_span(tile_rows), of_span(tile_cols), of_span(tile_count), of_span(send_blocks)]
    )
    is_mine = parity == core
    info = jnp.where(is_mine, own_info, swap(own_info))
    info = jnp.concatenate(
        [info, core.astype(jnp.int32)[None], parity.astype(jnp.int32)[None], spot.astype(jnp.int32)[None]]
    )
    dense, flipped, x0, g0 = call(
        functools.partial(prepare_body, tiles_max, nblocks),
        (
            jax.ShapeDtypeStruct((rows, rows + 2 * size), BF16),
            jax.ShapeDtypeStruct((rows, rows), BF16),
            jax.ShapeDtypeStruct((rows, width), BF16),
            jax.ShapeDtypeStruct((rows, width), BF16),
        ),
        [smem()] + [vmem()] * 6,
        [pltpu.VMEM((nblocks, nblocks + 2, size, size), F32)],
        10**6,
        4 * 10**6,
    )(info, own_x, swap(own_x), own_g, swap(own_g), own_t, swap(own_t))

    mine, dense = lax.optimization_barrier((mine, dense))
    got = swap(mine)

    mix, slope, fresh_out = call(
        functools.partial(forward_body, tiles_max),
        (
            jax.ShapeDtypeStruct((depth, rows, width), BF16),
            jax.ShapeDtypeStruct((depth, rows, width), F32),
            jax.ShapeDtypeStruct((depth, size, width), BF16),
        ),
        [smem()] * 2 + [hbm()] * 2 + [vmem()] * 2,
        [
            pltpu.VMEM((rows + 2 * size, width), BF16),
            pltpu.VMEM((rows, rows + 2 * size), BF16),
            pltpu.VMEM((rows, width), BF16),
            pltpu.VMEM((rows, width), F32),
            pltpu.SemaphoreType.DMA((2,)),
        ],
        1400 * 10**6,
        10**7,
    )(info, rates, dense, x0, mine, got)

    fresh_in = exchange(fresh_out, "section")

    few = half // CHIPS_X
    spare = width // depth + width // depth // 2
    *terms, columns = call(
        functools.partial(backward_body, tiles_max),
        (jax.ShapeDtypeStruct((depth * few, width), BF16),) * CHIPS_X
        + (jax.ShapeDtypeStruct((depth, spare, width), BF16),),
        [smem()] * 2 + [vmem()] * 6,
        [
            pltpu.VMEM((rows, width), BF16),
            pltpu.VMEM((rows, width), F32),
            pltpu.VMEM((rows, width), F32),
            pltpu.VMEM((half, width), BF16),
        ],
        100,
        100,
    )(info, rates, flipped, g0, mine, got, mix, slope)

    hop = CORES * chips_y
    pieces = [terms[0]] + [
        lax.ppermute(terms[k], "dom", [(i, (i + k * hop) % doms) for i in range(doms)])
        for k in range(1, CHIPS_X)
    ]
    parcel = call(
        merge_body,
        jax.ShapeDtypeStruct((depth, spare + few, width), BF16),
        [vmem()] * (CHIPS_X + 1),
        [],
        100,
        100,
    )(*pieces, columns)
    parcel, fresh_in = lax.optimization_barrier((parcel, fresh_in))

    arrived = exchange(parcel, "section")

    stays, leaves = call(
        part_body,
        (jax.ShapeDtypeStruct((spans, size, width), BF16),) * 2,
        [smem(), vmem()],
        [],
        100,
        100,
    )(core_ref, fresh_in)
    comes = lax.ppermute(
        leaves, "dom", [(i, (i - 1) % doms if i % 2 == 0 else (i + 1) % doms) for i in range(doms)]
    )
    along_x = [
        [(x * chips_y + y) * CORES + j for x in range(CHIPS_X)]
        for y in range(chips_y)
        for j in range(CORES)
    ]
    along_y = [
        [(x * chips_y + y) * CORES + j for y in range(chips_y)]
        for x in range(CHIPS_X)
        for j in range(CORES)
    ]
    pairs = [[CORES * i + j for j in range(CORES)] for i in range(chips)]
    scale = 1.0 / math.sqrt(spans * rows * doms)
    piece = arrived[:, spare:, :].astype(F32).sum(axis=0).astype(BF16)
    copies = jnp.broadcast_to(piece[None], (chips_y,) + piece.shape)
    copies, arrived, comes = lax.optimization_barrier((copies, arrived, comes))
    piece = exchange(copies, "dom", along_y).astype(F32).sum(axis=0) * scale
    copies = jnp.broadcast_to(piece[None], (CHIPS_X,) + piece.shape)
    piece = exchange(copies, "dom", along_x).reshape(half, width)
    weight_grad = lax.all_gather(piece, "dom", axis_index_groups=pairs, tiled=True)[None]

    fresh = call(
        fresh_body,
        jax.ShapeDtypeStruct((1, spans, 2 * size, width), BF16),
        [smem(), vmem(), vmem()],
        [],
        100,
        100,
    )(core_ref, stays, comes)

    initial_grad = call(
        unpack_body,
        jax.ShapeDtypeStruct((spans, width // depth, rows), F32),
        [smem(), vmem()],
        [],
        100,
        100,
    )(core_ref, arrived)
    return (weight_grad, fresh, initial_grad.transpose(0, 2, 1))


def solution(mesh):
    placed = (
        P(None, "dom", None),
        P(None, "dom", None),
        P("section", None, None),
        P("section", None, "dom", None),
        P(None, "dom", None, None),
        P(None, "dom"),
        P(None, "dom"),
        P(None, "dom"),
        P(None, "dom"),
    )
    return jax.shard_map(
        shards,
        mesh=mesh,
        in_specs=placed,
        out_specs=(
            P("section", None, None),
            P("section", None, "dom", None),
            P(None, "dom", "section"),
        ),
        check_vma=False,
    )
```

```python
import functools
import math

import jax
import jax.numpy as jnp
from jax import lax
from jax.experimental import pallas as pl
from jax.experimental.pallas import tpu as pltpu
from jax.sharding import PartitionSpec as P

ALPHA = 0.1
LAMBDA_RATE = 0.5
CORES = 2
CHIPS_X = 4
LARGE = 56
F32 = jnp.float32
BF16 = jnp.bfloat16


def vmem():
    return pl.BlockSpec(memory_space=pltpu.VMEM)


def smem():
    return pl.BlockSpec(memory_space=pltpu.SMEM)


def anywhere():
    return pl.BlockSpec(memory_space=pl.ANY)


def call(body, out_shape, in_specs, scratch, flops, moved, place=vmem, mib=24):
    return pl.pallas_call(
        body,
        out_shape=out_shape,
        in_specs=in_specs,
        out_specs=jax.tree.map(lambda _: place(), out_shape),
        scratch_shapes=scratch,
        compiler_params=pltpu.CompilerParams(vmem_limit_bytes=mib * 1024 * 1024),
        cost_estimate=pl.CostEstimate(flops=flops, bytes_accessed=moved, transcendentals=0),
    )


def slots_body(core_ref, halo, weight, out, sems):
    spans = halo.shape[0]
    core = core_ref[0]
    copies = [pltpu.make_async_copy(halo, out.at[core], sems.at[0])]
    for span in range(spans):
        copies.append(
            pltpu.make_async_copy(weight.at[0], out.at[1 - core, span], sems.at[1 + span])
        )
    for copy in copies:
        copy.start()
    for copy in copies:
        copy.wait()


def prepare_body(
    tiles_max, nblocks, info, own_x, got_x, own_g, got_g, own_t, got_t, job, acc
):
    size = acc.shape[-1]
    core = info[2 * tiles_max + 3]
    mine = info[2 * tiles_max + 4] == core
    acc[...] = jnp.zeros_like(acc)

    def add(slot, carry):
        row = info[slot]
        col = info[tiles_max + slot]
        col = jnp.where(col < nblocks, col, nblocks + jnp.where(col - nblocks == core, 0, 1))
        tile = jnp.where(mine, own_t[slot], got_t[slot])
        acc[row, col] += tile.astype(F32)
        return carry

    lax.fori_loop(0, info[2 * tiles_max], add, 0)
    for row in range(nblocks):
        for col in range(nblocks + 2):
            block = acc[row, col]
            job[row * size : (row + 1) * size, col * size : (col + 1) * size] = block.astype(BF16)
            if col < nblocks:
                lane = (nblocks + 2 + row) * size
                job[col * size : (col + 1) * size, lane : lane + size] = block.T.astype(BF16)
    lane = (2 * nblocks + 2) * size
    width = own_x.shape[1]
    job[:, lane : lane + width] = jnp.where(mine, own_x[...], got_x[...])
    job[:, lane + width : lane + 2 * width] = jnp.where(mine, own_g[...], got_g[...])


def weight_of(core, parity, mine, got, layer):
    own = mine[CORES * layer + 1 - parity]
    other = got[CORES * layer + 1 - parity]
    top = jnp.where(core == 0, own, other)
    bottom = jnp.where(core == 0, other, own)
    return jnp.concatenate([top, bottom], axis=0)


def chain_body(
    tiles_max, info, rates, job, mine, got, fresh, terms, columns,
    grad, ext, base, mixes, slopes, acc, last
):
    rows, width = base.shape
    wide = ext.shape[0]
    dense = slice(0, wide)
    flipped = slice(wide, wide + rows)
    inputs = slice(wide + rows, wide + rows + width)
    outer = slice(wide + rows + width, wide + rows + 2 * width)
    depth, size, _ = fresh.shape
    half = mine.shape[1]
    few = terms.shape[1] // depth
    core = info[2 * tiles_max + 3]
    parity = info[2 * tiles_max + 4]
    send = jnp.where(core == 0, info[2 * tiles_max + 1], info[2 * tiles_max + 2])
    ext[0:rows, :] = job[:, inputs]
    base[...] = ALPHA * job[:, inputs].astype(F32)
    grad[...] = job[:, outer]
    acc[...] = jnp.zeros_like(acc)

    def forward(layer, carry):
        rate = rates[layer]
        start = pl.multiple_of(send * size, size)
        fresh[layer] = ext[pl.ds(start, size), :]
        ext[rows : rows + half, :] = mine[CORES * layer + parity]
        ext[rows + half : rows + 2 * half, :] = got[CORES * layer + parity]
        agg = jnp.dot(job[:, dense], ext[...], preferred_element_type=F32)
        mix = ((1.0 - ALPHA) * agg + base[...]).astype(BF16)
        mixes[layer] = mix
        weight = weight_of(core, parity, mine, got, layer)
        pre = (1.0 - rate) * mix.astype(F32) + rate * jnp.dot(
            mix, weight, preferred_element_type=F32
        )
        gate = 0.5 * jnp.tanh(0.5 * pre) + 0.5
        silu = pre * gate
        slopes[layer] = gate + silu * (1.0 - gate)
        ext[0:rows, :] = silu.astype(BF16)
        return carry

    lax.fori_loop(0, depth, forward, 0)

    def backward(index, carry):
        layer = depth - 1 - index
        rate = rates[layer]
        delta = (grad[...].astype(F32) * slopes[layer]).astype(BF16)
        start = pl.multiple_of(core * half, half)
        part = mixes[layer, :, pl.ds(start, half)]
        weight = weight_of(core, parity, mine, got, layer)
        dmix = (1.0 - rate) * delta.astype(F32) + rate * lax.dot_general(
            delta, weight, (((1,), (1,)), ((), ())), preferred_element_type=F32
        )
        acc[...] += dmix
        back = jnp.dot(job[:, flipped], dmix.astype(BF16), preferred_element_type=F32)
        gx = (1.0 - ALPHA) * back
        grad[...] = gx.astype(BF16)
        dweight = lax.dot_general(
            part, delta, (((0,), (0,)), ((), ())), preferred_element_type=F32
        ).astype(BF16)
        row = pl.multiple_of(layer * few, few)
        for piece in range(CHIPS_X):
            terms[piece, pl.ds(row, few), :] = dweight[piece * few : (piece + 1) * few]

        @pl.when(layer == 0)
        def _():
            last[...] = gx

        return carry

    lax.fori_loop(0, depth, backward, 0)
    dinput = (ALPHA * acc[...] + last[...]).T.astype(BF16)
    share = width // depth
    hop = share // 2
    for part in range(depth):
        piece = dinput[part * share : (part + 1) * share]
        columns[part, :share, :] = piece[:, :width]
        columns[part, share:, : width // 2] = piece[:hop, width:]
        columns[part, share:, width // 2 :] = piece[hop:, width:]


def merge_body(pieces, fresh, columns, parcel):
    depth, size, _ = fresh.shape
    few = pieces.shape[1] // depth
    middle = size + columns.shape[1]
    for layer in range(depth):
        parcel[layer, :size, :] = fresh[layer]
        parcel[layer, size:middle, :] = columns[layer]
        rows = slice(layer * few, (layer + 1) * few)
        total = pieces[0, rows, :].astype(F32)
        for chip in range(1, pieces.shape[0]):
            total += pieces[chip, rows, :].astype(F32)
        parcel[layer, middle:, :] = total.astype(BF16)


def unpack_body(size, core_ref, arrived, out, stays, leaves):
    spans, share, _ = out.shape
    width = arrived.shape[-1]
    hop = share // 2
    base = core_ref[0] * spans
    away = (1 - core_ref[0]) * spans
    for span in range(spans):
        leaves[span] = arrived[base + span, :size, :]
        stays[span] = arrived[away + span, :size, :]
        top = arrived[base + span, size : size + share, :].astype(F32)
        low = arrived[base + span, size + share : size + share + hop, :].astype(F32)
        tail = jnp.concatenate([low[:, : width // 2], low[:, width // 2 :]], axis=0)
        out[span, :, :width] = top
        out[span, :, width:] = tail


def fresh_body(core_ref, stays, comes, out):
    size = stays.shape[1]
    first = core_ref[0] == 0
    for span in range(stays.shape[0]):
        own, other = stays[span], comes[span]
        out[0, span, :size, :] = jnp.where(first, other, own)
        out[0, span, size:, :] = jnp.where(first, own, other)


def assemble_body(spread, out):
    peers, few, _ = spread.shape
    for core in range(CORES):
        for chip in range(peers // CORES):
            row = (core * (peers // CORES) + chip) * few
            out[0, row : row + few, :] = spread[CORES * chip + core].astype(F32)


def swap(value):
    size = lax.axis_size("dom")
    return lax.ppermute(value, "dom", [(i, i ^ 1) for i in range(size)])


def exchange(value, axis, groups=None):
    return lax.all_to_all(value, axis, 0, 0, tiled=True, axis_index_groups=groups)


def shards(
    initial_embed,
    out_cotangent,
    layer_weights,
    stale_halo,
    tile_values,
    tile_rows,
    tile_cols,
    tile_count,
    send_blocks,
):
    section = lax.axis_index("section")
    depth = lax.axis_size("section")
    doms = lax.axis_size("dom")
    core = lax.axis_index("dom") % CORES
    spans, rows, width = initial_embed.shape
    tiles_max, size = tile_values.shape[1], tile_values.shape[-1]
    nblocks = rows // size
    half = width // 2
    chips = doms // CORES
    span = section % spans
    parity = section // spans
    rates = jnp.log(LAMBDA_RATE / (jnp.arange(depth, dtype=F32) + 1.0) + 1.0)

    slots = call(
        slots_body,
        jax.ShapeDtypeStruct((CORES, spans, CORES, size, width), BF16),
        [smem(), anywhere(), anywhere()],
        [pltpu.SemaphoreType.DMA((1 + spans,))],
        10**5,
        10**6,
        anywhere,
        LARGE,
    )(
        core.astype(jnp.int32)[None],
        stale_halo.reshape(spans, CORES, size, width),
        layer_weights.reshape(1, CORES, half, width),
    ).reshape(depth * CORES, size, width)
    column = [
        [z * doms + CORES * i + j for z in range(depth) for j in range(CORES)] for i in range(chips)
    ]
    mine = exchange(slots, ("section", "dom"), column)

    def of_span(value):
        return lax.dynamic_index_in_dim(value, span, 0, keepdims=False)

    own_x, own_g, own_t = of_span(initial_embed), of_span(out_cotangent), of_span(tile_values)
    own_info = jnp.concatenate(
        [of_span(tile_rows), of_span(tile_cols), of_span(tile_count), of_span(send_blocks)]
    )
    is_mine = parity == core
    info = jnp.where(is_mine, own_info, swap(own_info))
    info = jnp.concatenate(
        [info, core.astype(jnp.int32)[None], parity.astype(jnp.int32)[None]]
    )
    wide = rows + 2 * size
    job = call(
        functools.partial(prepare_body, tiles_max, nblocks),
        jax.ShapeDtypeStruct((rows, wide + rows + 2 * width), BF16),
        [smem()] + [vmem()] * 6,
        [pltpu.VMEM((nblocks, nblocks + 2, size, size), F32)],
        10**6,
        4 * 10**6,
    )(info, own_x, swap(own_x), own_g, swap(own_g), own_t, swap(own_t))

    mine, job = lax.optimization_barrier((mine, job))
    got = swap(mine)

    few = half // CHIPS_X
    spare = width // depth + width // depth // 2
    fresh_out, terms, columns = call(
        functools.partial(chain_body, tiles_max),
        (
            jax.ShapeDtypeStruct((depth, size, width), BF16),
            jax.ShapeDtypeStruct((CHIPS_X, depth * few, width), BF16),
            jax.ShapeDtypeStruct((depth, spare, width), BF16),
        ),
        [smem()] * 2 + [vmem()] * 3,
        [
            pltpu.VMEM((rows, width), BF16),
            pltpu.VMEM((wide, width), BF16),
            pltpu.VMEM((rows, width), F32),
            pltpu.VMEM((depth, rows, width), BF16),
            pltpu.VMEM((depth, rows, width), F32),
            pltpu.VMEM((rows, width), F32),
            pltpu.VMEM((rows, width), F32),
        ],
        2800 * 10**6,
        10**7,
    )(info, rates, job, mine, got)

    chips_y = chips // CHIPS_X
    along_x = [
        [(x * chips_y + y) * CORES + j for x in range(CHIPS_X)]
        for y in range(chips_y)
        for j in range(CORES)
    ]
    along_y = [
        [(x * chips_y + y) * CORES + j for y in range(chips_y)]
        for x in range(CHIPS_X)
        for j in range(CORES)
    ]
    plane = [
        [(x * chips_y + y) * CORES + j for x in range(CHIPS_X) for j in range(CORES)]
        for y in range(chips_y)
    ]
    pieces = exchange(terms, "dom", along_x)
    parcel = call(
        merge_body,
        jax.ShapeDtypeStruct((depth, size + spare + few, width), BF16),
        [vmem()] * 3,
        [],
        10**6,
        10**6,
    )(pieces, fresh_out, columns)

    arrived = exchange(parcel, "section")
    scale = 1.0 / math.sqrt(spans * rows * doms)
    piece = arrived[:, size + spare :, :].astype(F32).sum(axis=0).astype(BF16)
    copies = jnp.broadcast_to(piece[None], (chips_y,) + piece.shape)
    copies, arrived = lax.optimization_barrier((copies, arrived))
    piece = exchange(copies, "dom", along_y).astype(F32).sum(axis=0) * scale
    piece = piece.astype(BF16)
    copies = jnp.broadcast_to(piece[None], (CHIPS_X * CORES,) + piece.shape)
    spread = exchange(copies, "dom", plane)
    weight_grad = call(
        assemble_body,
        jax.ShapeDtypeStruct((1, width, width), F32),
        [vmem()],
        [],
        100,
        100,
    )(spread)

    initial_grad, stays, leaves = call(
        functools.partial(unpack_body, size),
        (
            jax.ShapeDtypeStruct((spans, width // depth, rows), F32),
            jax.ShapeDtypeStruct((spans, size, width), BF16),
            jax.ShapeDtypeStruct((spans, size, width), BF16),
        ),
        [smem(), vmem()],
        [],
        100,
        100,
    )(core.astype(jnp.int32)[None], arrived)
    comes = lax.ppermute(
        leaves, "dom", [(i, (i - 1) % doms if i % 2 == 0 else (i + 1) % doms) for i in range(doms)]
    )
    fresh = call(
        fresh_body,
        jax.ShapeDtypeStruct((1, spans, 2 * size, width), BF16),
        [smem(), vmem(), vmem()],
        [],
        100,
        100,
    )(core.astype(jnp.int32)[None], stays, comes)
    return (weight_grad, fresh, initial_grad.transpose(0, 2, 1))


def solution(mesh):
    placed = (
        P(None, "dom", None),
        P(None, "dom", None),
        P("section", None, None),
        P("section", None, "dom", None),
        P(None, "dom", None, None),
        P(None, "dom"),
        P(None, "dom"),
        P(None, "dom"),
        P(None, "dom"),
    )
    return jax.shard_map(
        shards,
        mesh=mesh,
        in_specs=placed,
        out_specs=(
            P("section", None, None),
            P("section", None, "dom", None),
            P(None, "dom", "section"),
        ),
        check_vma=False,
    )
```

```python
import functools
import math

import jax
import jax.numpy as jnp
from jax import lax
from jax.experimental import pallas as pl
from jax.experimental.pallas import tpu as pltpu
from jax.sharding import PartitionSpec as P

ALPHA = 0.1
LAMBDA_RATE = 0.5
CORES = 2
CHIPS_X = 4
LARGE = 56
F32 = jnp.float32
BF16 = jnp.bfloat16


def vmem():
    return pl.BlockSpec(memory_space=pltpu.VMEM)


def smem():
    return pl.BlockSpec(memory_space=pltpu.SMEM)


def anywhere():
    return pl.BlockSpec(memory_space=pl.ANY)


def call(body, out_shape, in_specs, scratch, flops, moved, place=vmem, mib=24):
    return pl.pallas_call(
        body,
        out_shape=out_shape,
        in_specs=in_specs,
        out_specs=jax.tree.map(lambda _: place(), out_shape),
        scratch_shapes=scratch,
        compiler_params=pltpu.CompilerParams(vmem_limit_bytes=mib * 1024 * 1024),
        cost_estimate=pl.CostEstimate(flops=flops, bytes_accessed=moved, transcendentals=0),
    )


def slots_body(core_ref, halo_far, weight_far, out, halo, weight, fetched, sent):
    spans = halo.shape[0]
    core = core_ref[0]
    weight_in = pltpu.make_async_copy(weight_far, weight, fetched.at[0])
    halo_in = pltpu.make_async_copy(halo_far, halo, fetched.at[1])
    weight_in.start()
    halo_in.start()
    copies = [
        pltpu.make_async_copy(weight, out.at[1 - core, span], sent.at[1 + span])
        for span in range(spans)
    ] + [pltpu.make_async_copy(halo, out.at[core], sent.at[0])]
    weight_in.wait()
    for copy in copies[:-1]:
        copy.start()
    halo_in.wait()
    copies[-1].start()
    for copy in copies:
        copy.wait()


def prepare_body(
    tiles_max, nblocks, info, own_x, got_x, own_g, got_g, own_t, got_t, job, acc
):
    size = acc.shape[-1]
    core = info[2 * tiles_max + 3]
    mine = info[2 * tiles_max + 4] == core
    acc[...] = jnp.zeros_like(acc)

    def add(slot, carry):
        row = info[slot]
        col = info[tiles_max + slot]
        col = jnp.where(col < nblocks, col, nblocks + jnp.where(col - nblocks == core, 0, 1))
        tile = jnp.where(mine, own_t[slot], got_t[slot])
        acc[row, col] += tile.astype(F32)
        return carry

    lax.fori_loop(0, info[2 * tiles_max], add, 0)
    for row in range(nblocks):
        for col in range(nblocks + 2):
            block = acc[row, col]
            job[row * size : (row + 1) * size, col * size : (col + 1) * size] = block.astype(BF16)
            if col < nblocks:
                lane = (nblocks + 2 + row) * size
                job[col * size : (col + 1) * size, lane : lane + size] = block.T.astype(BF16)
    lane = (2 * nblocks + 2) * size
    width = own_x.shape[1]
    job[:, lane : lane + width] = jnp.where(mine, own_x[...], got_x[...])
    job[:, lane + width : lane + 2 * width] = jnp.where(mine, own_g[...], got_g[...])


def weight_of(core, parity, mine, got, layer):
    own = mine[CORES * layer + 1 - parity]
    other = got[CORES * layer + 1 - parity]
    top = jnp.where(core == 0, own, other)
    bottom = jnp.where(core == 0, other, own)
    return jnp.concatenate([top, bottom], axis=0)


def chain_body(
    tiles_max, info, rates, job, mine, got, fresh, terms, columns,
    grad, ext, base, mixes, slopes, acc, last
):
    rows, width = base.shape
    wide = ext.shape[0]
    dense = slice(0, wide)
    flipped = slice(wide, wide + rows)
    inputs = slice(wide + rows, wide + rows + width)
    outer = slice(wide + rows + width, wide + rows + 2 * width)
    depth, size, _ = fresh.shape
    half = mine.shape[1]
    few = terms.shape[1] // depth
    core = info[2 * tiles_max + 3]
    parity = info[2 * tiles_max + 4]
    send = jnp.where(core == 0, info[2 * tiles_max + 1], info[2 * tiles_max + 2])
    ext[0:rows, :] = job[:, inputs]
    base[...] = ALPHA * job[:, inputs].astype(F32)
    grad[...] = job[:, outer]
    acc[...] = jnp.zeros_like(acc)

    def forward(layer, carry):
        rate = rates[layer]
        start = pl.multiple_of(send * size, size)
        fresh[layer] = ext[pl.ds(start, size), :]
        ext[rows : rows + half, :] = mine[CORES * layer + parity]
        ext[rows + half : rows + 2 * half, :] = got[CORES * layer + parity]
        agg = jnp.dot(job[:, dense], ext[...], preferred_element_type=F32)
        mix = ((1.0 - ALPHA) * agg + base[...]).astype(BF16)
        mixes[layer] = mix
        weight = weight_of(core, parity, mine, got, layer)
        pre = (1.0 - rate) * mix.astype(F32) + rate * jnp.dot(
            mix, weight, preferred_element_type=F32
        )
        gate = 0.5 * jnp.tanh(0.5 * pre) + 0.5
        silu = pre * gate
        slopes[layer] = gate + silu * (1.0 - gate)
        ext[0:rows, :] = silu.astype(BF16)
        return carry

    lax.fori_loop(0, depth, forward, 0)

    def backward(index, carry):
        layer = depth - 1 - index
        rate = rates[layer]
        delta = (grad[...].astype(F32) * slopes[layer]).astype(BF16)
        start = pl.multiple_of(core * half, half)
        part = mixes[layer, :, pl.ds(start, half)]
        weight = weight_of(core, parity, mine, got, layer)
        dmix = (1.0 - rate) * delta.astype(F32) + rate * lax.dot_general(
            delta, weight, (((1,), (1,)), ((), ())), preferred_element_type=F32
        )
        acc[...] += dmix
        back = jnp.dot(job[:, flipped], dmix.astype(BF16), preferred_element_type=F32)
        gx = (1.0 - ALPHA) * back
        grad[...] = gx.astype(BF16)
        dweight = lax.dot_general(
            part, delta, (((0,), (0,)), ((), ())), preferred_element_type=F32
        ).astype(BF16)
        row = pl.multiple_of(layer * few, few)
        for piece in range(CHIPS_X):
            terms[piece, pl.ds(row, few), :] = dweight[piece * few : (piece + 1) * few]

        @pl.when(layer == 0)
        def _():
            last[...] = gx

        return carry

    lax.fori_loop(0, depth, backward, 0)
    dinput = (ALPHA * acc[...] + last[...]).T.astype(BF16)
    share = width // depth
    hop = share // 2
    for part in range(depth):
        piece = dinput[part * share : (part + 1) * share]
        columns[part, :share, :] = piece[:, :width]
        columns[part, share:, : width // 2] = piece[:hop, width:]
        columns[part, share:, width // 2 :] = piece[hop:, width:]


def merge_body(pieces, fresh, columns, parcel):
    depth, size, _ = fresh.shape
    few = pieces.shape[1] // depth
    middle = size + columns.shape[1]
    for layer in range(depth):
        parcel[layer, :size, :] = fresh[layer]
        parcel[layer, size:middle, :] = columns[layer]
        rows = slice(layer * few, (layer + 1) * few)
        total = pieces[0, rows, :].astype(F32)
        for chip in range(1, pieces.shape[0]):
            total += pieces[chip, rows, :].astype(F32)
        parcel[layer, middle:, :] = total.astype(BF16)


def unpack_body(size, core_ref, arrived, out, stays, leaves):
    spans, share, _ = out.shape
    width = arrived.shape[-1]
    hop = share // 2
    base = core_ref[0] * spans
    away = (1 - core_ref[0]) * spans
    for span in range(spans):
        leaves[span] = arrived[base + span, :size, :]
        stays[span] = arrived[away + span, :size, :]
        top = arrived[base + span, size : size + share, :].astype(F32)
        low = arrived[base + span, size + share : size + share + hop, :].astype(F32)
        tail = jnp.concatenate([low[:, : width // 2], low[:, width // 2 :]], axis=0)
        out[span, :, :width] = top
        out[span, :, width:] = tail


def fresh_body(core_ref, stays, comes, out):
    size = stays.shape[1]
    first = core_ref[0] == 0
    for span in range(stays.shape[0]):
        own, other = stays[span], comes[span]
        out[0, span, :size, :] = jnp.where(first, other, own)
        out[0, span, size:, :] = jnp.where(first, own, other)


def assemble_body(spread, out):
    peers, few, _ = spread.shape
    for core in range(CORES):
        for chip in range(peers // CORES):
            row = (core * (peers // CORES) + chip) * few
            out[0, row : row + few, :] = spread[CORES * chip + core].astype(F32)


def swap(value):
    size = lax.axis_size("dom")
    return lax.ppermute(value, "dom", [(i, i ^ 1) for i in range(size)])


def exchange(value, axis, groups=None):
    return lax.all_to_all(value, axis, 0, 0, tiled=True, axis_index_groups=groups)


def shards(
    initial_embed,
    out_cotangent,
    layer_weights,
    stale_halo,
    tile_values,
    tile_rows,
    tile_cols,
    tile_count,
    send_blocks,
):
    section = lax.axis_index("section")
    depth = lax.axis_size("section")
    doms = lax.axis_size("dom")
    core = lax.axis_index("dom") % CORES
    spans, rows, width = initial_embed.shape
    tiles_max, size = tile_values.shape[1], tile_values.shape[-1]
    nblocks = rows // size
    half = width // 2
    chips = doms // CORES
    span = section % spans
    parity = section // spans
    rates = jnp.log(LAMBDA_RATE / (jnp.arange(depth, dtype=F32) + 1.0) + 1.0)

    slots = call(
        slots_body,
        jax.ShapeDtypeStruct((CORES, spans, CORES, size, width), BF16),
        [smem(), anywhere(), anywhere()],
        [
            pltpu.VMEM((spans, CORES, size, width), BF16),
            pltpu.VMEM((CORES, half, width), BF16),
            pltpu.SemaphoreType.DMA((2,)),
            pltpu.SemaphoreType.DMA((1 + spans,)),
        ],
        10**5,
        10**6,
        anywhere,
        LARGE,
    )(
        core.astype(jnp.int32)[None],
        stale_halo.reshape(spans, CORES, size, width),
        layer_weights.reshape(CORES, half, width),
    ).reshape(depth * CORES, size, width)
    column = [
        [z * doms + CORES * i + j for z in range(depth) for j in range(CORES)] for i in range(chips)
    ]
    mine = exchange(slots, ("section", "dom"), column)

    def of_span(value):
        return lax.dynamic_index_in_dim(value, span, 0, keepdims=False)

    own_x, own_g, own_t = of_span(initial_embed), of_span(out_cotangent), of_span(tile_values)
    own_info = jnp.concatenate(
        [of_span(tile_rows), of_span(tile_cols), of_span(tile_count), of_span(send_blocks)]
    )
    is_mine = parity == core
    info = jnp.where(is_mine, own_info, swap(own_info))
    info = jnp.concatenate(
        [info, core.astype(jnp.int32)[None], parity.astype(jnp.int32)[None]]
    )
    wide = rows + 2 * size
    job = call(
        functools.partial(prepare_body, tiles_max, nblocks),
        jax.ShapeDtypeStruct((rows, wide + rows + 2 * width), BF16),
        [smem()] + [vmem()] * 6,
        [pltpu.VMEM((nblocks, nblocks + 2, size, size), F32)],
        10**6,
        4 * 10**6,
    )(info, own_x, swap(own_x), own_g, swap(own_g), own_t, swap(own_t))

    mine, job = lax.optimization_barrier((mine, job))
    got = swap(mine)

    few = half // CHIPS_X
    spare = width // depth + width // depth // 2
    fresh_out, terms, columns = call(
        functools.partial(chain_body, tiles_max),
        (
            jax.ShapeDtypeStruct((depth, size, width), BF16),
            jax.ShapeDtypeStruct((CHIPS_X, depth * few, width), BF16),
            jax.ShapeDtypeStruct((depth, spare, width), BF16),
        ),
        [smem()] * 2 + [vmem()] * 3,
        [
            pltpu.VMEM((rows, width), BF16),
            pltpu.VMEM((wide, width), BF16),
            pltpu.VMEM((rows, width), F32),
            pltpu.VMEM((depth, rows, width), BF16),
            pltpu.VMEM((depth, rows, width), F32),
            pltpu.VMEM((rows, width), F32),
            pltpu.VMEM((rows, width), F32),
        ],
        2800 * 10**6,
        10**7,
    )(info, rates, job, mine, got)

    chips_y = chips // CHIPS_X
    along_x = [
        [(x * chips_y + y) * CORES + j for x in range(CHIPS_X)]
        for y in range(chips_y)
        for j in range(CORES)
    ]
    along_y = [
        [(x * chips_y + y) * CORES + j for y in range(chips_y)]
        for x in range(CHIPS_X)
        for j in range(CORES)
    ]
    plane = [
        [(x * chips_y + y) * CORES + j for x in range(CHIPS_X) for j in range(CORES)]
        for y in range(chips_y)
    ]
    pieces = exchange(terms, "dom", along_x)
    parcel = call(
        merge_body,
        jax.ShapeDtypeStruct((depth, size + spare + few, width), BF16),
        [vmem()] * 3,
        [],
        10**6,
        10**6,
    )(pieces, fresh_out, columns)

    arrived = exchange(parcel, "section")
    scale = 1.0 / math.sqrt(spans * rows * doms)
    piece = arrived[:, size + spare :, :].astype(F32).sum(axis=0).astype(BF16)
    copies = jnp.broadcast_to(piece[None], (chips_y,) + piece.shape)
    copies, arrived = lax.optimization_barrier((copies, arrived))
    piece = exchange(copies, "dom", along_y).astype(F32).sum(axis=0) * scale
    piece = piece.astype(BF16)
    copies = jnp.broadcast_to(piece[None], (CHIPS_X * CORES,) + piece.shape)
    spread = exchange(copies, "dom", plane)
    weight_grad = call(
        assemble_body,
        jax.ShapeDtypeStruct((1, width, width), F32),
        [vmem()],
        [],
        100,
        100,
    )(spread)

    initial_grad, stays, leaves = call(
        functools.partial(unpack_body, size),
        (
            jax.ShapeDtypeStruct((spans, width // depth, rows), F32),
            jax.ShapeDtypeStruct((spans, size, width), BF16),
            jax.ShapeDtypeStruct((spans, size, width), BF16),
        ),
        [smem(), vmem()],
        [],
        100,
        100,
    )(core.astype(jnp.int32)[None], arrived)
    comes = lax.ppermute(
        leaves, "dom", [(i, (i - 1) % doms if i % 2 == 0 else (i + 1) % doms) for i in range(doms)]
    )
    fresh = call(
        fresh_body,
        jax.ShapeDtypeStruct((1, spans, 2 * size, width), BF16),
        [smem(), vmem(), vmem()],
        [],
        100,
        100,
    )(core.astype(jnp.int32)[None], stays, comes)
    return (weight_grad, fresh, initial_grad.transpose(0, 2, 1))


def solution(mesh):
    placed = (
        P(None, "dom", None),
        P(None, "dom", None),
        P("section", None, None),
        P("section", None, "dom", None),
        P(None, "dom", None, None),
        P(None, "dom"),
        P(None, "dom"),
        P(None, "dom"),
        P(None, "dom"),
    )
    return jax.shard_map(
        shards,
        mesh=mesh,
        in_specs=placed,
        out_specs=(
            P("section", None, None),
            P("section", None, "dom", None),
            P(None, "dom", "section"),
        ),
        check_vma=False,
    )
```

```python
import functools
import math

import jax
import jax.numpy as jnp
from jax import lax
from jax.experimental import pallas as pl
from jax.experimental.pallas import tpu as pltpu
from jax.sharding import PartitionSpec as P

ALPHA = 0.1
LAMBDA_RATE = 0.5
CORES = 2
CHIPS_X = 4
LARGE = 56
F32 = jnp.float32
BF16 = jnp.bfloat16


def vmem():
    return pl.BlockSpec(memory_space=pltpu.VMEM)


def smem():
    return pl.BlockSpec(memory_space=pltpu.SMEM)


def anywhere():
    return pl.BlockSpec(memory_space=pl.ANY)


def call(body, out_shape, in_specs, scratch, flops, moved, place=vmem, mib=24):
    return pl.pallas_call(
        body,
        out_shape=out_shape,
        in_specs=in_specs,
        out_specs=jax.tree.map(lambda _: place(), out_shape),
        scratch_shapes=scratch,
        compiler_params=pltpu.CompilerParams(vmem_limit_bytes=mib * 1024 * 1024),
        cost_estimate=pl.CostEstimate(flops=flops, bytes_accessed=moved, transcendentals=0),
    )


def slots_body(core_ref, halo_far, weight_far, out, halo, weight, fetched, sent):
    spans = halo.shape[0]
    core = core_ref[0]
    weight_in = pltpu.make_async_copy(weight_far, weight, fetched.at[0])
    halo_in = pltpu.make_async_copy(halo_far, halo, fetched.at[1])
    weight_in.start()
    halo_in.start()
    copies = [
        pltpu.make_async_copy(weight, out.at[1 - core, span], sent.at[1 + span])
        for span in range(spans)
    ] + [pltpu.make_async_copy(halo, out.at[core], sent.at[0])]
    weight_in.wait()
    for copy in copies[:-1]:
        copy.start()
    halo_in.wait()
    copies[-1].start()
    for copy in copies:
        copy.wait()


def prepare_body(
    tiles_max, nblocks, info, own_x, got_x, own_g, got_g, own_t, got_t, job, acc
):
    size = acc.shape[-1]
    core = info[2 * tiles_max + 3]
    mine = info[2 * tiles_max + 4] == core
    acc[...] = jnp.zeros_like(acc)

    def add(slot, carry):
        row = info[slot]
        col = info[tiles_max + slot]
        col = jnp.where(col < nblocks, col, nblocks + jnp.where(col - nblocks == core, 0, 1))
        tile = jnp.where(mine, own_t[slot], got_t[slot])
        acc[row, col] += tile.astype(F32)
        return carry

    lax.fori_loop(0, info[2 * tiles_max], add, 0)
    for row in range(nblocks):
        for col in range(nblocks + 2):
            block = acc[row, col]
            job[row * size : (row + 1) * size, col * size : (col + 1) * size] = block.astype(BF16)
            if col < nblocks:
                lane = (nblocks + 2 + row) * size
                job[col * size : (col + 1) * size, lane : lane + size] = block.T.astype(BF16)
    lane = (2 * nblocks + 2) * size
    width = own_x.shape[1]
    job[:, lane : lane + width] = jnp.where(mine, own_x[...], got_x[...])
    job[:, lane + width : lane + 2 * width] = jnp.where(mine, own_g[...], got_g[...])


def weight_of(core, parity, mine, got, layer):
    own = mine[CORES * layer + 1 - parity]
    other = got[CORES * layer + 1 - parity]
    top = jnp.where(core == 0, own, other)
    bottom = jnp.where(core == 0, other, own)
    return jnp.concatenate([top, bottom], axis=0)


def chain_body(
    tiles_max, info, rates, job, mine, got, fresh, terms, columns,
    grad, ext, base, mixes, slopes, acc, last
):
    rows, width = base.shape
    wide = ext.shape[0]
    dense = slice(0, wide)
    flipped = slice(wide, wide + rows)
    inputs = slice(wide + rows, wide + rows + width)
    outer = slice(wide + rows + width, wide + rows + 2 * width)
    depth, size, _ = fresh.shape
    half = mine.shape[1]
    few = terms.shape[1] // depth
    core = info[2 * tiles_max + 3]
    parity = info[2 * tiles_max + 4]
    send = jnp.where(core == 0, info[2 * tiles_max + 1], info[2 * tiles_max + 2])
    ext[0:rows, :] = job[:, inputs]
    base[...] = ALPHA * job[:, inputs].astype(F32)
    grad[...] = job[:, outer]
    acc[...] = jnp.zeros_like(acc)

    def forward(layer, carry):
        rate = rates[layer]
        start = pl.multiple_of(send * size, size)
        fresh[layer] = ext[pl.ds(start, size), :]
        ext[rows : rows + half, :] = mine[CORES * layer + parity]
        ext[rows + half : rows + 2 * half, :] = got[CORES * layer + parity]
        agg = jnp.dot(job[:, dense], ext[...], preferred_element_type=F32)
        mix = ((1.0 - ALPHA) * agg + base[...]).astype(BF16)
        mixes[layer] = mix
        weight = weight_of(core, parity, mine, got, layer)
        pre = (1.0 - rate) * mix.astype(F32) + rate * jnp.dot(
            mix, weight, preferred_element_type=F32
        )
        gate = 0.5 * jnp.tanh(0.5 * pre) + 0.5
        silu = pre * gate
        slopes[layer] = gate + silu * (1.0 - gate)
        ext[0:rows, :] = silu.astype(BF16)
        return carry

    lax.fori_loop(0, depth, forward, 0, unroll=True)

    def backward(index, carry):
        layer = depth - 1 - index
        rate = rates[layer]
        delta = (grad[...].astype(F32) * slopes[layer]).astype(BF16)
        start = pl.multiple_of(core * half, half)
        part = mixes[layer, :, pl.ds(start, half)]
        weight = weight_of(core, parity, mine, got, layer)
        dmix = (1.0 - rate) * delta.astype(F32) + rate * lax.dot_general(
            delta, weight, (((1,), (1,)), ((), ())), preferred_element_type=F32
        )
        acc[...] += dmix
        back = jnp.dot(job[:, flipped], dmix.astype(BF16), preferred_element_type=F32)
        gx = (1.0 - ALPHA) * back
        grad[...] = gx.astype(BF16)
        dweight = lax.dot_general(
            part, delta, (((0,), (0,)), ((), ())), preferred_element_type=F32
        ).astype(BF16)
        row = pl.multiple_of(layer * few, few)
        for piece in range(CHIPS_X):
            terms[piece, pl.ds(row, few), :] = dweight[piece * few : (piece + 1) * few]

        @pl.when(layer == 0)
        def _():
            last[...] = gx

        return carry

    lax.fori_loop(0, depth, backward, 0, unroll=True)
    dinput = (ALPHA * acc[...] + last[...]).T.astype(BF16)
    share = width // depth
    hop = share // 2
    for part in range(depth):
        piece = dinput[part * share : (part + 1) * share]
        columns[part, :share, :] = piece[:, :width]
        columns[part, share:, : width // 2] = piece[:hop, width:]
        columns[part, share:, width // 2 :] = piece[hop:, width:]


def merge_body(pieces, fresh, columns, parcel):
    depth, size, _ = fresh.shape
    few = pieces.shape[1] // depth
    middle = size + columns.shape[1]
    for layer in range(depth):
        parcel[layer, :size, :] = fresh[layer]
        parcel[layer, size:middle, :] = columns[layer]
        rows = slice(layer * few, (layer + 1) * few)
        total = pieces[0, rows, :].astype(F32)
        for chip in range(1, pieces.shape[0]):
            total += pieces[chip, rows, :].astype(F32)
        parcel[layer, middle:, :] = total.astype(BF16)


def unpack_body(size, core_ref, arrived, out, stays, leaves):
    spans, share, _ = out.shape
    width = arrived.shape[-1]
    hop = share // 2
    base = core_ref[0] * spans
    away = (1 - core_ref[0]) * spans
    for span in range(spans):
        leaves[span] = arrived[base + span, :size, :]
        stays[span] = arrived[away + span, :size, :]
        top = arrived[base + span, size : size + share, :].astype(F32)
        low = arrived[base + span, size + share : size + share + hop, :].astype(F32)
        tail = jnp.concatenate([low[:, : width // 2], low[:, width // 2 :]], axis=0)
        out[span, :, :width] = top
        out[span, :, width:] = tail


def fresh_body(core_ref, stays, comes, out):
    size = stays.shape[1]
    first = core_ref[0] == 0
    for span in range(stays.shape[0]):
        own, other = stays[span], comes[span]
        out[0, span, :size, :] = jnp.where(first, other, own)
        out[0, span, size:, :] = jnp.where(first, own, other)


def assemble_body(spread, out):
    peers, few, _ = spread.shape
    for core in range(CORES):
        for chip in range(peers // CORES):
            row = (core * (peers // CORES) + chip) * few
            out[0, row : row + few, :] = spread[CORES * chip + core].astype(F32)


def swap(value):
    size = lax.axis_size("dom")
    return lax.ppermute(value, "dom", [(i, i ^ 1) for i in range(size)])


def exchange(value, axis, groups=None):
    return lax.all_to_all(value, axis, 0, 0, tiled=True, axis_index_groups=groups)


def shards(
    initial_embed,
    out_cotangent,
    layer_weights,
    stale_halo,
    tile_values,
    tile_rows,
    tile_cols,
    tile_count,
    send_blocks,
):
    section = lax.axis_index("section")
    depth = lax.axis_size("section")
    doms = lax.axis_size("dom")
    core = lax.axis_index("dom") % CORES
    spans, rows, width = initial_embed.shape
    tiles_max, size = tile_values.shape[1], tile_values.shape[-1]
    nblocks = rows // size
    half = width // 2
    chips = doms // CORES
    span = section % spans
    parity = section // spans
    rates = jnp.log(LAMBDA_RATE / (jnp.arange(depth, dtype=F32) + 1.0) + 1.0)

    slots = call(
        slots_body,
        jax.ShapeDtypeStruct((CORES, spans, CORES, size, width), BF16),
        [smem(), anywhere(), anywhere()],
        [
            pltpu.VMEM((spans, CORES, size, width), BF16),
            pltpu.VMEM((CORES, half, width), BF16),
            pltpu.SemaphoreType.DMA((2,)),
            pltpu.SemaphoreType.DMA((1 + spans,)),
        ],
        10**5,
        10**6,
        anywhere,
        LARGE,
    )(
        core.astype(jnp.int32)[None],
        stale_halo.reshape(spans, CORES, size, width),
        layer_weights.reshape(CORES, half, width),
    ).reshape(depth * CORES, size, width)
    column = [
        [z * doms + CORES * i + j for z in range(depth) for j in range(CORES)] for i in range(chips)
    ]
    mine = exchange(slots, ("section", "dom"), column)

    def of_span(value):
        return lax.dynamic_index_in_dim(value, span, 0, keepdims=False)

    own_x, own_g, own_t = of_span(initial_embed), of_span(out_cotangent), of_span(tile_values)
    own_info = jnp.concatenate(
        [of_span(tile_rows), of_span(tile_cols), of_span(tile_count), of_span(send_blocks)]
    )
    is_mine = parity == core
    info = jnp.where(is_mine, own_info, swap(own_info))
    info = jnp.concatenate(
        [info, core.astype(jnp.int32)[None], parity.astype(jnp.int32)[None]]
    )
    wide = rows + 2 * size
    job = call(
        functools.partial(prepare_body, tiles_max, nblocks),
        jax.ShapeDtypeStruct((rows, wide + rows + 2 * width), BF16),
        [smem()] + [vmem()] * 6,
        [pltpu.VMEM((nblocks, nblocks + 2, size, size), F32)],
        10**6,
        4 * 10**6,
    )(info, own_x, swap(own_x), own_g, swap(own_g), own_t, swap(own_t))

    mine, job = lax.optimization_barrier((mine, job))
    got = swap(mine)

    few = half // CHIPS_X
    spare = width // depth + width // depth // 2
    fresh_out, terms, columns = call(
        functools.partial(chain_body, tiles_max),
        (
            jax.ShapeDtypeStruct((depth, size, width), BF16),
            jax.ShapeDtypeStruct((CHIPS_X, depth * few, width), BF16),
            jax.ShapeDtypeStruct((depth, spare, width), BF16),
        ),
        [smem()] * 2 + [vmem()] * 3,
        [
            pltpu.VMEM((rows, width), BF16),
            pltpu.VMEM((wide, width), BF16),
            pltpu.VMEM((rows, width), F32),
            pltpu.VMEM((depth, rows, width), BF16),
            pltpu.VMEM((depth, rows, width), F32),
            pltpu.VMEM((rows, width), F32),
            pltpu.VMEM((rows, width), F32),
        ],
        2800 * 10**6,
        10**7,
    )(info, rates, job, mine, got)

    chips_y = chips // CHIPS_X
    along_x = [
        [(x * chips_y + y) * CORES + j for x in range(CHIPS_X)]
        for y in range(chips_y)
        for j in range(CORES)
    ]
    along_y = [
        [(x * chips_y + y) * CORES + j for y in range(chips_y)]
        for x in range(CHIPS_X)
        for j in range(CORES)
    ]
    plane = [
        [(x * chips_y + y) * CORES + j for x in range(CHIPS_X) for j in range(CORES)]
        for y in range(chips_y)
    ]
    pieces = exchange(terms, "dom", along_x)
    parcel = call(
        merge_body,
        jax.ShapeDtypeStruct((depth, size + spare + few, width), BF16),
        [vmem()] * 3,
        [],
        10**6,
        10**6,
    )(pieces, fresh_out, columns)

    arrived = exchange(parcel, "section")
    scale = 1.0 / math.sqrt(spans * rows * doms)
    piece = arrived[:, size + spare :, :].astype(F32).sum(axis=0).astype(BF16)
    copies = jnp.broadcast_to(piece[None], (chips_y,) + piece.shape)
    copies, arrived = lax.optimization_barrier((copies, arrived))
    piece = exchange(copies, "dom", along_y).astype(F32).sum(axis=0) * scale
    initial_grad, stays, leaves = call(
        functools.partial(unpack_body, size),
        (
            jax.ShapeDtypeStruct((spans, width // depth, rows), F32),
            jax.ShapeDtypeStruct((spans, size, width), BF16),
            jax.ShapeDtypeStruct((spans, size, width), BF16),
        ),
        [smem(), vmem()],
        [],
        100,
        100,
    )(core.astype(jnp.int32)[None], arrived)
    piece = piece.astype(BF16)
    copies = jnp.broadcast_to(piece[None], (CHIPS_X * CORES,) + piece.shape)
    copies, leaves = lax.optimization_barrier((copies, leaves))
    spread = exchange(copies, "dom", plane)
    comes = lax.ppermute(
        leaves, "dom", [(i, (i - 1) % doms if i % 2 == 0 else (i + 1) % doms) for i in range(doms)]
    )
    fresh = call(
        fresh_body,
        jax.ShapeDtypeStruct((1, spans, 2 * size, width), BF16),
        [smem(), vmem(), vmem()],
        [],
        100,
        100,
    )(core.astype(jnp.int32)[None], stays, comes)
    spread, fresh = lax.optimization_barrier((spread, fresh))
    weight_grad = call(
        assemble_body,
        jax.ShapeDtypeStruct((1, width, width), F32),
        [vmem()],
        [],
        100,
        100,
    )(spread)
    return (weight_grad, fresh, initial_grad.transpose(0, 2, 1))


def solution(mesh):
    placed = (
        P(None, "dom", None),
        P(None, "dom", None),
        P("section", None, None),
        P("section", None, "dom", None),
        P(None, "dom", None, None),
        P(None, "dom"),
        P(None, "dom"),
        P(None, "dom"),
        P(None, "dom"),
    )
    return jax.shard_map(
        shards,
        mesh=mesh,
        in_specs=placed,
        out_specs=(
            P("section", None, None),
            P("section", None, "dom", None),
            P(None, "dom", "section"),
        ),
        check_vma=False,
    )
```

```python
import functools
import math

import jax
import jax.numpy as jnp
from jax import lax
from jax.experimental import pallas as pl
from jax.experimental.pallas import tpu as pltpu
from jax.sharding import PartitionSpec as P

ALPHA = 0.1
LAMBDA_RATE = 0.5
CORES = 2
CHIPS_X = 4
LARGE = 56
F32 = jnp.float32
BF16 = jnp.bfloat16


def vmem():
    return pl.BlockSpec(memory_space=pltpu.VMEM)


def smem():
    return pl.BlockSpec(memory_space=pltpu.SMEM)


def anywhere():
    return pl.BlockSpec(memory_space=pl.ANY)


def call(body, out_shape, in_specs, scratch, flops, moved, place=vmem, mib=24):
    return pl.pallas_call(
        body,
        out_shape=out_shape,
        in_specs=in_specs,
        out_specs=jax.tree.map(lambda _: place(), out_shape),
        scratch_shapes=scratch,
        compiler_params=pltpu.CompilerParams(vmem_limit_bytes=mib * 1024 * 1024),
        cost_estimate=pl.CostEstimate(flops=flops, bytes_accessed=moved, transcendentals=0),
    )


def slots_body(core_ref, halo_far, weight_far, out, halo, weight, fetched, sent):
    spans = halo.shape[0]
    core = core_ref[0]
    weight_in = pltpu.make_async_copy(weight_far, weight, fetched.at[0])
    halo_in = pltpu.make_async_copy(halo_far, halo, fetched.at[1])
    weight_in.start()
    halo_in.start()
    copies = [
        pltpu.make_async_copy(weight, out.at[1 - core, span], sent.at[1 + span])
        for span in range(spans)
    ] + [pltpu.make_async_copy(halo, out.at[core], sent.at[0])]
    weight_in.wait()
    for copy in copies[:-1]:
        copy.start()
    halo_in.wait()
    copies[-1].start()
    for copy in copies:
        copy.wait()


def prepare_body(
    tiles_max, nblocks, info, own_x, got_x, own_g, got_g, own_t, got_t, job, acc
):
    size = acc.shape[-1]
    core = info[2 * tiles_max + 3]
    mine = info[2 * tiles_max + 4] == core
    acc[...] = jnp.zeros_like(acc)

    def add(slot, carry):
        row = info[slot]
        col = info[tiles_max + slot]
        col = jnp.where(col < nblocks, col, nblocks + jnp.where(col - nblocks == core, 0, 1))
        tile = jnp.where(mine, own_t[slot], got_t[slot])
        acc[row, col] += tile.astype(F32)
        return carry

    lax.fori_loop(0, info[2 * tiles_max], add, 0)
    for row in range(nblocks):
        for col in range(nblocks + 2):
            block = acc[row, col]
            job[row * size : (row + 1) * size, col * size : (col + 1) * size] = block.astype(BF16)
            if col < nblocks:
                lane = (nblocks + 2 + row) * size
                job[col * size : (col + 1) * size, lane : lane + size] = block.T.astype(BF16)
    lane = (2 * nblocks + 2) * size
    width = own_x.shape[1]
    job[:, lane : lane + width] = jnp.where(mine, own_x[...], got_x[...])
    job[:, lane + width : lane + 2 * width] = jnp.where(mine, own_g[...], got_g[...])


def weight_of(core, parity, mine, got, layer):
    own = mine[CORES * layer + 1 - parity]
    other = got[CORES * layer + 1 - parity]
    top = jnp.where(core == 0, own, other)
    bottom = jnp.where(core == 0, other, own)
    return jnp.concatenate([top, bottom], axis=0)


def chain_body(
    tiles_max, info, rates, job, mine, got, fresh, terms, columns,
    grad, ext, base, mixes, slopes, acc, last
):
    rows, width = base.shape
    wide = ext.shape[0]
    dense = slice(0, wide)
    flipped = slice(wide, wide + rows)
    inputs = slice(wide + rows, wide + rows + width)
    outer = slice(wide + rows + width, wide + rows + 2 * width)
    depth, size, _ = fresh.shape
    half = mine.shape[1]
    few = terms.shape[1] // depth
    core = info[2 * tiles_max + 3]
    parity = info[2 * tiles_max + 4]
    send = jnp.where(core == 0, info[2 * tiles_max + 1], info[2 * tiles_max + 2])
    ext[0:rows, :] = job[:, inputs]
    base[...] = ALPHA * job[:, inputs].astype(F32)
    grad[...] = job[:, outer]
    acc[...] = jnp.zeros_like(acc)

    def forward(layer, carry):
        rate = rates[layer]
        start = pl.multiple_of(send * size, size)
        fresh[layer] = ext[pl.ds(start, size), :]
        ext[rows : rows + half, :] = mine[CORES * layer + parity]
        ext[rows + half : rows + 2 * half, :] = got[CORES * layer + parity]
        agg = jnp.dot(job[:, dense], ext[...], preferred_element_type=F32)
        mix = ((1.0 - ALPHA) * agg + base[...]).astype(BF16)
        mixes[layer] = mix
        weight = weight_of(core, parity, mine, got, layer)
        pre = (1.0 - rate) * mix.astype(F32) + rate * jnp.dot(
            mix, weight, preferred_element_type=F32
        )
        gate = 0.5 * jnp.tanh(0.5 * pre) + 0.5
        silu = pre * gate
        slopes[layer] = gate + silu * (1.0 - gate)
        ext[0:rows, :] = silu.astype(BF16)
        return carry

    lax.fori_loop(0, depth, forward, 0, unroll=True)

    def backward(index, carry):
        layer = depth - 1 - index
        rate = rates[layer]
        delta = (grad[...].astype(F32) * slopes[layer]).astype(BF16)
        start = pl.multiple_of(core * half, half)
        part = mixes[layer, :, pl.ds(start, half)]
        weight = weight_of(core, parity, mine, got, layer)
        dmix = (1.0 - rate) * delta.astype(F32) + rate * lax.dot_general(
            delta, weight, (((1,), (1,)), ((), ())), preferred_element_type=F32
        )
        acc[...] += dmix
        back = jnp.dot(job[:, flipped], dmix.astype(BF16), preferred_element_type=F32)
        gx = (1.0 - ALPHA) * back
        grad[...] = gx.astype(BF16)
        dweight = lax.dot_general(
            part, delta, (((0,), (0,)), ((), ())), preferred_element_type=F32
        ).astype(BF16)
        row = pl.multiple_of(layer * few, few)
        for piece in range(CHIPS_X):
            terms[piece, pl.ds(row, few), :] = dweight[piece * few : (piece + 1) * few]

        @pl.when(layer == 0)
        def _():
            last[...] = gx

        return carry

    lax.fori_loop(0, depth, backward, 0, unroll=True)
    dinput = (ALPHA * acc[...] + last[...]).T.astype(BF16)
    share = width // depth
    hop = share // 2
    for part in range(depth):
        piece = dinput[part * share : (part + 1) * share]
        columns[part, :share, :] = piece[:, :width]
        columns[part, share:, : width // 2] = piece[:hop, width:]
        columns[part, share:, width // 2 :] = piece[hop:, width:]


def merge_body(pieces, fresh, columns, parcel):
    depth, size, _ = fresh.shape
    few = pieces.shape[1] // depth
    middle = size + columns.shape[1]
    for layer in range(depth):
        parcel[layer, :size, :] = fresh[layer]
        parcel[layer, size:middle, :] = columns[layer]
        rows = slice(layer * few, (layer + 1) * few)
        total = pieces[0, rows, :].astype(F32)
        for chip in range(1, pieces.shape[0]):
            total += pieces[chip, rows, :].astype(F32)
        parcel[layer, middle:, :] = total.astype(BF16)


def unpack_body(size, core_ref, arrived, out, stays, leaves):
    spans, share, _ = out.shape
    width = arrived.shape[-1]
    hop = share // 2
    base = core_ref[0] * spans
    away = (1 - core_ref[0]) * spans
    for span in range(spans):
        leaves[span] = arrived[base + span, :size, :]
        stays[span] = arrived[away + span, :size, :]
        top = arrived[base + span, size : size + share, :].astype(F32)
        low = arrived[base + span, size + share : size + share + hop, :].astype(F32)
        tail = jnp.concatenate([low[:, : width // 2], low[:, width // 2 :]], axis=0)
        out[span, :, :width] = top
        out[span, :, width:] = tail


def fresh_body(core_ref, stays, comes, out):
    size = stays.shape[1]
    first = core_ref[0] == 0
    for span in range(stays.shape[0]):
        own, other = stays[span], comes[span]
        out[0, span, :size, :] = jnp.where(first, other, own)
        out[0, span, size:, :] = jnp.where(first, own, other)


def assemble_body(spread, out):
    peers, few, _ = spread.shape
    for core in range(CORES):
        for chip in range(peers // CORES):
            row = (core * (peers // CORES) + chip) * few
            out[0, row : row + few, :] = spread[CORES * chip + core].astype(F32)


def swap(value):
    size = lax.axis_size("dom")
    return lax.ppermute(value, "dom", [(i, i ^ 1) for i in range(size)])


def exchange(value, axis, groups=None):
    return lax.all_to_all(value, axis, 0, 0, tiled=True, axis_index_groups=groups)


def shards(
    initial_embed,
    out_cotangent,
    layer_weights,
    stale_halo,
    tile_values,
    tile_rows,
    tile_cols,
    tile_count,
    send_blocks,
):
    section = lax.axis_index("section")
    depth = lax.axis_size("section")
    doms = lax.axis_size("dom")
    core = lax.axis_index("dom") % CORES
    spans, rows, width = initial_embed.shape
    tiles_max, size = tile_values.shape[1], tile_values.shape[-1]
    nblocks = rows // size
    half = width // 2
    chips = doms // CORES
    span = section % spans
    parity = section // spans
    rates = jnp.log(LAMBDA_RATE / (jnp.arange(depth, dtype=F32) + 1.0) + 1.0)

    slots = call(
        slots_body,
        jax.ShapeDtypeStruct((CORES, spans, CORES, size, width), BF16),
        [smem(), anywhere(), anywhere()],
        [
            pltpu.VMEM((spans, CORES, size, width), BF16),
            pltpu.VMEM((CORES, half, width), BF16),
            pltpu.SemaphoreType.DMA((2,)),
            pltpu.SemaphoreType.DMA((1 + spans,)),
        ],
        10**5,
        10**6,
        anywhere,
        LARGE,
    )(
        core.astype(jnp.int32)[None],
        stale_halo.reshape(spans, CORES, size, width),
        layer_weights.reshape(CORES, half, width),
    ).reshape(depth * CORES, size, width)
    column = [
        [z * doms + CORES * i + j for z in range(depth) for j in range(CORES)] for i in range(chips)
    ]
    mine = exchange(slots, ("section", "dom"), column)

    def of_span(value):
        return lax.dynamic_index_in_dim(value, span, 0, keepdims=False)

    own_x, own_g, own_t = of_span(initial_embed), of_span(out_cotangent), of_span(tile_values)
    own_info = jnp.concatenate(
        [of_span(tile_rows), of_span(tile_cols), of_span(tile_count), of_span(send_blocks)]
    )
    is_mine = parity == core
    info = jnp.where(is_mine, own_info, swap(own_info))
    info = jnp.concatenate(
        [info, core.astype(jnp.int32)[None], parity.astype(jnp.int32)[None]]
    )
    wide = rows + 2 * size
    job = call(
        functools.partial(prepare_body, tiles_max, nblocks),
        jax.ShapeDtypeStruct((rows, wide + rows + 2 * width), BF16),
        [smem()] + [vmem()] * 6,
        [pltpu.VMEM((nblocks, nblocks + 2, size, size), F32)],
        10**6,
        4 * 10**6,
    )(info, own_x, swap(own_x), own_g, swap(own_g), own_t, swap(own_t))

    mine, job = lax.optimization_barrier((mine, job))
    got = swap(mine)

    few = half // CHIPS_X
    spare = width // depth + width // depth // 2
    fresh_out, terms, columns = call(
        functools.partial(chain_body, tiles_max),
        (
            jax.ShapeDtypeStruct((depth, size, width), BF16),
            jax.ShapeDtypeStruct((CHIPS_X, depth * few, width), BF16),
            jax.ShapeDtypeStruct((depth, spare, width), BF16),
        ),
        [smem()] * 2 + [vmem()] * 3,
        [
            pltpu.VMEM((rows, width), BF16),
            pltpu.VMEM((wide, width), BF16),
            pltpu.VMEM((rows, width), F32),
            pltpu.VMEM((depth, rows, width), BF16),
            pltpu.VMEM((depth, rows, width), F32),
            pltpu.VMEM((rows, width), F32),
            pltpu.VMEM((rows, width), F32),
        ],
        2800 * 10**6,
        10**7,
    )(info, rates, job, mine, got)

    chips_y = chips // CHIPS_X
    along_x = [
        [(x * chips_y + y) * CORES + j for x in range(CHIPS_X)]
        for y in range(chips_y)
        for j in range(CORES)
    ]
    along_y = [
        [(x * chips_y + y) * CORES + j for y in range(chips_y)]
        for x in range(CHIPS_X)
        for j in range(CORES)
    ]
    plane = [
        [(x * chips_y + y) * CORES + j for x in range(CHIPS_X) for j in range(CORES)]
        for y in range(chips_y)
    ]
    pieces = exchange(terms, "dom", along_x)
    parcel = call(
        merge_body,
        jax.ShapeDtypeStruct((depth, size + spare + few, width), BF16),
        [vmem()] * 3,
        [],
        10**6,
        10**6,
    )(pieces, fresh_out, columns)

    arrived = exchange(parcel, "section")
    scale = 1.0 / math.sqrt(spans * rows * doms)
    piece = arrived[:, size + spare :, :].astype(F32).sum(axis=0).astype(BF16)
    copies = jnp.broadcast_to(piece[None], (chips_y,) + piece.shape)
    copies, arrived = lax.optimization_barrier((copies, arrived))
    piece = exchange(copies, "dom", along_y).astype(F32).sum(axis=0) * scale
    piece = piece.astype(BF16)
    copies = jnp.broadcast_to(piece[None], (CHIPS_X * CORES,) + piece.shape)
    spread = exchange(copies, "dom", plane)
    weight_grad = call(
        assemble_body,
        jax.ShapeDtypeStruct((1, width, width), F32),
        [vmem()],
        [],
        100,
        100,
    )(spread)

    initial_grad, stays, leaves = call(
        functools.partial(unpack_body, size),
        (
            jax.ShapeDtypeStruct((spans, width // depth, rows), F32),
            jax.ShapeDtypeStruct((spans, size, width), BF16),
            jax.ShapeDtypeStruct((spans, size, width), BF16),
        ),
        [smem(), vmem()],
        [],
        100,
        100,
    )(core.astype(jnp.int32)[None], arrived)
    comes = lax.ppermute(
        leaves, "dom", [(i, (i - 1) % doms if i % 2 == 0 else (i + 1) % doms) for i in range(doms)]
    )
    fresh = call(
        fresh_body,
        jax.ShapeDtypeStruct((1, spans, 2 * size, width), BF16),
        [smem(), vmem(), vmem()],
        [],
        100,
        100,
    )(core.astype(jnp.int32)[None], stays, comes)
    return (weight_grad, fresh, initial_grad.transpose(0, 2, 1))


def solution(mesh):
    placed = (
        P(None, "dom", None),
        P(None, "dom", None),
        P("section", None, None),
        P("section", None, "dom", None),
        P(None, "dom", None, None),
        P(None, "dom"),
        P(None, "dom"),
        P(None, "dom"),
        P(None, "dom"),
    )
    return jax.shard_map(
        shards,
        mesh=mesh,
        in_specs=placed,
        out_specs=(
            P("section", None, None),
            P("section", None, "dom", None),
            P(None, "dom", "section"),
        ),
        check_vma=False,
    )
```

```python
import functools
import math

import jax
import jax.numpy as jnp
from jax import lax
from jax.experimental import pallas as pl
from jax.experimental.pallas import tpu as pltpu
from jax.sharding import PartitionSpec as P

ALPHA = 0.1
LAMBDA_RATE = 0.5
CORES = 2
CHIPS_X = 4
NEAR_Y = 2
PARTS = CHIPS_X * NEAR_Y
LARGE = 56
F32 = jnp.float32
BF16 = jnp.bfloat16


def vmem():
    return pl.BlockSpec(memory_space=pltpu.VMEM)


def smem():
    return pl.BlockSpec(memory_space=pltpu.SMEM)


def anywhere():
    return pl.BlockSpec(memory_space=pl.ANY)


def call(body, out_shape, in_specs, scratch, flops, moved, place=vmem, mib=24):
    return pl.pallas_call(
        body,
        out_shape=out_shape,
        in_specs=in_specs,
        out_specs=jax.tree.map(lambda _: place(), out_shape),
        scratch_shapes=scratch,
        compiler_params=pltpu.CompilerParams(vmem_limit_bytes=mib * 1024 * 1024),
        cost_estimate=pl.CostEstimate(flops=flops, bytes_accessed=moved, transcendentals=0),
    )


def slots_body(core_ref, halo_far, weight_far, out, halo, weight, fetched, sent):
    spans = halo.shape[0]
    core = core_ref[0]
    weight_in = pltpu.make_async_copy(weight_far, weight, fetched.at[0])
    halo_in = pltpu.make_async_copy(halo_far, halo, fetched.at[1])
    weight_in.start()
    halo_in.start()
    copies = [
        pltpu.make_async_copy(weight, out.at[1 - core, span], sent.at[1 + span])
        for span in range(spans)
    ] + [pltpu.make_async_copy(halo, out.at[core], sent.at[0])]
    weight_in.wait()
    for copy in copies[:-1]:
        copy.start()
    halo_in.wait()
    copies[-1].start()
    for copy in copies:
        copy.wait()


def prepare_body(
    tiles_max, nblocks, info, own_x, got_x, own_g, got_g, own_t, got_t, job, acc
):
    size = acc.shape[-1]
    core = info[2 * tiles_max + 3]
    mine = info[2 * tiles_max + 4] == core
    acc[...] = jnp.zeros_like(acc)

    def add(slot, carry):
        row = info[slot]
        col = info[tiles_max + slot]
        col = jnp.where(col < nblocks, col, nblocks + jnp.where(col - nblocks == core, 0, 1))
        tile = jnp.where(mine, own_t[slot], got_t[slot])
        acc[row, col] += tile.astype(F32)
        return carry

    lax.fori_loop(0, info[2 * tiles_max], add, 0)
    for row in range(nblocks):
        for col in range(nblocks + 2):
            block = acc[row, col]
            job[row * size : (row + 1) * size, col * size : (col + 1) * size] = block.astype(BF16)
            if col < nblocks:
                lane = (nblocks + 2 + row) * size
                job[col * size : (col + 1) * size, lane : lane + size] = block.T.astype(BF16)
    lane = (2 * nblocks + 2) * size
    width = own_x.shape[1]
    job[:, lane : lane + width] = jnp.where(mine, own_x[...], got_x[...])
    job[:, lane + width : lane + 2 * width] = jnp.where(mine, own_g[...], got_g[...])


def weight_of(core, parity, mine, got, layer):
    own = mine[CORES * layer + 1 - parity]
    other = got[CORES * layer + 1 - parity]
    top = jnp.where(core == 0, own, other)
    bottom = jnp.where(core == 0, other, own)
    return jnp.concatenate([top, bottom], axis=0)


def chain_body(
    tiles_max, info, rates, job, mine, got, fresh, terms, columns,
    grad, ext, base, mixes, slopes, acc, last
):
    rows, width = base.shape
    wide = ext.shape[0]
    dense = slice(0, wide)
    flipped = slice(wide, wide + rows)
    inputs = slice(wide + rows, wide + rows + width)
    outer = slice(wide + rows + width, wide + rows + 2 * width)
    depth, size, _ = fresh.shape
    half = mine.shape[1]
    few = terms.shape[1] // depth
    core = info[2 * tiles_max + 3]
    parity = info[2 * tiles_max + 4]
    send = jnp.where(core == 0, info[2 * tiles_max + 1], info[2 * tiles_max + 2])
    ext[0:rows, :] = job[:, inputs]
    base[...] = ALPHA * job[:, inputs].astype(F32)
    grad[...] = job[:, outer]
    acc[...] = jnp.zeros_like(acc)

    def forward(layer, carry):
        rate = rates[layer]
        start = pl.multiple_of(send * size, size)
        fresh[layer] = ext[pl.ds(start, size), :]
        ext[rows : rows + half, :] = mine[CORES * layer + parity]
        ext[rows + half : rows + 2 * half, :] = got[CORES * layer + parity]
        agg = jnp.dot(job[:, dense], ext[...], preferred_element_type=F32)
        mix = ((1.0 - ALPHA) * agg + base[...]).astype(BF16)
        mixes[layer] = mix
        weight = weight_of(core, parity, mine, got, layer)
        pre = (1.0 - rate) * mix.astype(F32) + rate * jnp.dot(
            mix, weight, preferred_element_type=F32
        )
        gate = 0.5 * jnp.tanh(0.5 * pre) + 0.5
        silu = pre * gate
        slopes[layer] = gate + silu * (1.0 - gate)
        ext[0:rows, :] = silu.astype(BF16)
        return carry

    lax.fori_loop(0, depth, forward, 0, unroll=True)

    def backward(index, carry):
        layer = depth - 1 - index
        rate = rates[layer]
        delta = (grad[...].astype(F32) * slopes[layer]).astype(BF16)
        start = pl.multiple_of(core * half, half)
        part = mixes[layer, :, pl.ds(start, half)]
        weight = weight_of(core, parity, mine, got, layer)
        dmix = (1.0 - rate) * delta.astype(F32) + rate * lax.dot_general(
            delta, weight, (((1,), (1,)), ((), ())), preferred_element_type=F32
        )
        acc[...] += dmix
        back = jnp.dot(job[:, flipped], dmix.astype(BF16), preferred_element_type=F32)
        gx = (1.0 - ALPHA) * back
        grad[...] = gx.astype(BF16)
        dweight = lax.dot_general(
            part, delta, (((0,), (0,)), ((), ())), preferred_element_type=F32
        ).astype(BF16)
        row = pl.multiple_of(layer * few, few)
        for piece in range(PARTS):
            terms[piece, pl.ds(row, few), :] = dweight[piece * few : (piece + 1) * few]

        @pl.when(layer == 0)
        def _():
            last[...] = gx

        return carry

    lax.fori_loop(0, depth, backward, 0, unroll=True)
    dinput = (ALPHA * acc[...] + last[...]).T.astype(BF16)
    share = width // depth
    hop = share // 2
    for part in range(depth):
        piece = dinput[part * share : (part + 1) * share]
        columns[part, :share, :] = piece[:, :width]
        columns[part, share:, : width // 2] = piece[:hop, width:]
        columns[part, share:, width // 2 :] = piece[hop:, width:]


def merge_body(pieces, fresh, columns, parcel):
    depth, size, _ = fresh.shape
    few = pieces.shape[1] // depth
    middle = size + columns.shape[1]
    for layer in range(depth):
        parcel[layer, :size, :] = fresh[layer]
        parcel[layer, size:middle, :] = columns[layer]
        rows = slice(layer * few, (layer + 1) * few)
        total = pieces[0, rows, :].astype(F32)
        for chip in range(1, pieces.shape[0]):
            total += pieces[chip, rows, :].astype(F32)
        parcel[layer, middle:, :] = total.astype(BF16)


def unpack_body(size, core_ref, arrived, out, stays, leaves):
    spans, share, _ = out.shape
    width = arrived.shape[-1]
    hop = share // 2
    base = core_ref[0] * spans
    away = (1 - core_ref[0]) * spans
    for span in range(spans):
        leaves[span] = arrived[base + span, :size, :]
        stays[span] = arrived[away + span, :size, :]
        top = arrived[base + span, size : size + share, :].astype(F32)
        low = arrived[base + span, size + share : size + share + hop, :].astype(F32)
        tail = jnp.concatenate([low[:, : width // 2], low[:, width // 2 :]], axis=0)
        out[span, :, :width] = top
        out[span, :, width:] = tail


def fresh_body(core_ref, stays, comes, out):
    size = stays.shape[1]
    first = core_ref[0] == 0
    for span in range(stays.shape[0]):
        own, other = stays[span], comes[span]
        out[0, span, :size, :] = jnp.where(first, other, own)
        out[0, span, size:, :] = jnp.where(first, own, other)


def assemble_body(spread, out):
    peers, few, _ = spread.shape
    for core in range(CORES):
        for chip in range(peers // CORES):
            row = (core * (peers // CORES) + chip) * few
            out[0, row : row + few, :] = spread[CORES * chip + core].astype(F32)


def swap(value):
    size = lax.axis_size("dom")
    return lax.ppermute(value, "dom", [(i, i ^ 1) for i in range(size)])


def exchange(value, axis, groups=None):
    return lax.all_to_all(value, axis, 0, 0, tiled=True, axis_index_groups=groups)


def shards(
    initial_embed,
    out_cotangent,
    layer_weights,
    stale_halo,
    tile_values,
    tile_rows,
    tile_cols,
    tile_count,
    send_blocks,
):
    section = lax.axis_index("section")
    depth = lax.axis_size("section")
    doms = lax.axis_size("dom")
    core = lax.axis_index("dom") % CORES
    spans, rows, width = initial_embed.shape
    tiles_max, size = tile_values.shape[1], tile_values.shape[-1]
    nblocks = rows // size
    half = width // 2
    chips = doms // CORES
    span = section % spans
    parity = section // spans
    rates = jnp.log(LAMBDA_RATE / (jnp.arange(depth, dtype=F32) + 1.0) + 1.0)

    slots = call(
        slots_body,
        jax.ShapeDtypeStruct((CORES, spans, CORES, size, width), BF16),
        [smem(), anywhere(), anywhere()],
        [
            pltpu.VMEM((spans, CORES, size, width), BF16),
            pltpu.VMEM((CORES, half, width), BF16),
            pltpu.SemaphoreType.DMA((2,)),
            pltpu.SemaphoreType.DMA((1 + spans,)),
        ],
        10**5,
        10**6,
        anywhere,
        LARGE,
    )(
        core.astype(jnp.int32)[None],
        stale_halo.reshape(spans, CORES, size, width),
        layer_weights.reshape(CORES, half, width),
    ).reshape(depth * CORES, size, width)
    column = [
        [z * doms + CORES * i + j for z in range(depth) for j in range(CORES)] for i in range(chips)
    ]
    mine = exchange(slots, ("section", "dom"), column)

    def of_span(value):
        return lax.dynamic_index_in_dim(value, span, 0, keepdims=False)

    own_x, own_g, own_t = of_span(initial_embed), of_span(out_cotangent), of_span(tile_values)
    own_info = jnp.concatenate(
        [of_span(tile_rows), of_span(tile_cols), of_span(tile_count), of_span(send_blocks)]
    )
    is_mine = parity == core
    info = jnp.where(is_mine, own_info, swap(own_info))
    info = jnp.concatenate(
        [info, core.astype(jnp.int32)[None], parity.astype(jnp.int32)[None]]
    )
    wide = rows + 2 * size
    job = call(
        functools.partial(prepare_body, tiles_max, nblocks),
        jax.ShapeDtypeStruct((rows, wide + rows + 2 * width), BF16),
        [smem()] + [vmem()] * 6,
        [pltpu.VMEM((nblocks, nblocks + 2, size, size), F32)],
        10**6,
        4 * 10**6,
    )(info, own_x, swap(own_x), own_g, swap(own_g), own_t, swap(own_t))

    mine, job = lax.optimization_barrier((mine, job))
    got = swap(mine)

    few = half // PARTS
    spare = width // depth + width // depth // 2
    fresh_out, terms, columns = call(
        functools.partial(chain_body, tiles_max),
        (
            jax.ShapeDtypeStruct((depth, size, width), BF16),
            jax.ShapeDtypeStruct((PARTS, depth * few, width), BF16),
            jax.ShapeDtypeStruct((depth, spare, width), BF16),
        ),
        [smem()] * 2 + [vmem()] * 3,
        [
            pltpu.VMEM((rows, width), BF16),
            pltpu.VMEM((wide, width), BF16),
            pltpu.VMEM((rows, width), F32),
            pltpu.VMEM((depth, rows, width), BF16),
            pltpu.VMEM((depth, rows, width), F32),
            pltpu.VMEM((rows, width), F32),
            pltpu.VMEM((rows, width), F32),
        ],
        2800 * 10**6,
        10**7,
    )(info, rates, job, mine, got)

    chips_y = chips // CHIPS_X
    far_y = chips_y // NEAR_Y

    def dom_of(x, far, near, j):
        return (x * chips_y + far * NEAR_Y + near) * CORES + j

    xs, nears, fars, cores = range(CHIPS_X), range(NEAR_Y), range(far_y), range(CORES)
    block = [[dom_of(x, f, n, j) for x in xs for n in nears] for f in fars for j in cores]
    along_y = [[dom_of(x, f, n, j) for f in fars] for x in xs for n in nears for j in cores]
    plane = [[dom_of(x, f, n, j) for x in xs for n in nears for j in cores] for f in fars]
    pieces = exchange(terms, "dom", block)
    parcel = call(
        merge_body,
        jax.ShapeDtypeStruct((depth, size + spare + few, width), BF16),
        [vmem()] * 3,
        [],
        10**6,
        10**6,
    )(pieces, fresh_out, columns)

    arrived = exchange(parcel, "section")
    scale = 1.0 / math.sqrt(spans * rows * doms)
    piece = arrived[:, size + spare :, :].astype(F32).sum(axis=0).astype(BF16)
    copies = jnp.broadcast_to(piece[None], (far_y,) + piece.shape)
    copies, arrived = lax.optimization_barrier((copies, arrived))
    piece = exchange(copies, "dom", along_y).astype(F32).sum(axis=0) * scale
    piece = piece.astype(BF16)
    copies = jnp.broadcast_to(piece[None], (PARTS * CORES,) + piece.shape)
    spread = exchange(copies, "dom", plane)
    weight_grad = call(
        assemble_body,
        jax.ShapeDtypeStruct((1, width, width), F32),
        [vmem()],
        [],
        100,
        100,
    )(spread)

    initial_grad, stays, leaves = call(
        functools.partial(unpack_body, size),
        (
            jax.ShapeDtypeStruct((spans, width // depth, rows), F32),
            jax.ShapeDtypeStruct((spans, size, width), BF16),
            jax.ShapeDtypeStruct((spans, size, width), BF16),
        ),
        [smem(), vmem()],
        [],
        100,
        100,
    )(core.astype(jnp.int32)[None], arrived)
    comes = lax.ppermute(
        leaves, "dom", [(i, (i - 1) % doms if i % 2 == 0 else (i + 1) % doms) for i in range(doms)]
    )
    fresh = call(
        fresh_body,
        jax.ShapeDtypeStruct((1, spans, 2 * size, width), BF16),
        [smem(), vmem(), vmem()],
        [],
        100,
        100,
    )(core.astype(jnp.int32)[None], stays, comes)
    return (weight_grad, fresh, initial_grad.transpose(0, 2, 1))


def solution(mesh):
    placed = (
        P(None, "dom", None),
        P(None, "dom", None),
        P("section", None, None),
        P("section", None, "dom", None),
        P(None, "dom", None, None),
        P(None, "dom"),
        P(None, "dom"),
        P(None, "dom"),
        P(None, "dom"),
    )
    return jax.shard_map(
        shards,
        mesh=mesh,
        in_specs=placed,
        out_specs=(
            P("section", None, None),
            P("section", None, "dom", None),
            P(None, "dom", "section"),
        ),
        check_vma=False,
    )
```

```python
import functools
import math

import jax
import jax.numpy as jnp
from jax import lax
from jax.experimental import pallas as pl
from jax.experimental.pallas import tpu as pltpu
from jax.sharding import PartitionSpec as P

ALPHA = 0.1
LAMBDA_RATE = 0.5
CORES = 2
CHIPS_X = 4
NEAR_Y = 2
PARTS = CHIPS_X * NEAR_Y
LARGE = 56
F32 = jnp.float32
BF16 = jnp.bfloat16


def vmem():
    return pl.BlockSpec(memory_space=pltpu.VMEM)


def smem():
    return pl.BlockSpec(memory_space=pltpu.SMEM)


def anywhere():
    return pl.BlockSpec(memory_space=pl.ANY)


def call(body, out_shape, in_specs, scratch, flops, moved, place=vmem, mib=24):
    return pl.pallas_call(
        body,
        out_shape=out_shape,
        in_specs=in_specs,
        out_specs=jax.tree.map(lambda _: place(), out_shape),
        scratch_shapes=scratch,
        compiler_params=pltpu.CompilerParams(vmem_limit_bytes=mib * 1024 * 1024),
        cost_estimate=pl.CostEstimate(flops=flops, bytes_accessed=moved, transcendentals=0),
    )


def slots_body(core_ref, halo_far, weight_far, out, halo, weight, fetched, sent):
    spans = halo.shape[0]
    core = core_ref[0]
    weight_in = pltpu.make_async_copy(weight_far, weight, fetched.at[0])
    halo_in = pltpu.make_async_copy(halo_far, halo, fetched.at[1])
    weight_in.start()
    halo_in.start()
    copies = [
        pltpu.make_async_copy(weight, out.at[1 - core, span], sent.at[1 + span])
        for span in range(spans)
    ] + [pltpu.make_async_copy(halo, out.at[core], sent.at[0])]
    weight_in.wait()
    for copy in copies[:-1]:
        copy.start()
    halo_in.wait()
    copies[-1].start()
    for copy in copies:
        copy.wait()


def prepare_body(
    tiles_max, nblocks, info, own_x, got_x, own_g, got_g, own_t, got_t, job, acc
):
    size = acc.shape[-1]
    core = info[2 * tiles_max + 3]
    mine = info[2 * tiles_max + 4] == core
    acc[...] = jnp.zeros_like(acc)

    def add(slot, carry):
        row = info[slot]
        col = info[tiles_max + slot]
        col = jnp.where(col < nblocks, col, nblocks + jnp.where(col - nblocks == core, 0, 1))
        tile = jnp.where(mine, own_t[slot], got_t[slot])
        acc[row, col] += tile.astype(F32)
        return carry

    lax.fori_loop(0, info[2 * tiles_max], add, 0)
    for row in range(nblocks):
        for col in range(nblocks + 2):
            block = acc[row, col]
            job[row * size : (row + 1) * size, col * size : (col + 1) * size] = block.astype(BF16)
            if col < nblocks:
                lane = (nblocks + 2 + row) * size
                job[col * size : (col + 1) * size, lane : lane + size] = block.T.astype(BF16)
    lane = (2 * nblocks + 2) * size
    width = own_x.shape[1]
    job[:, lane : lane + width] = jnp.where(mine, own_x[...], got_x[...])
    job[:, lane + width : lane + 2 * width] = jnp.where(mine, own_g[...], got_g[...])


def weight_of(core, parity, mine, got, layer):
    own = mine[CORES * layer + 1 - parity]
    other = got[CORES * layer + 1 - parity]
    top = jnp.where(core == 0, own, other)
    bottom = jnp.where(core == 0, other, own)
    return jnp.concatenate([top, bottom], axis=0)


def chain_body(
    tiles_max, info, rates, job, mine, got, fresh, terms, columns,
    grad, ext, base, mixes, slopes, acc, last, turned
):
    rows, width = base.shape
    wide = ext.shape[0]
    dense = slice(0, wide)
    flipped = slice(wide, wide + rows)
    inputs = slice(wide + rows, wide + rows + width)
    outer = slice(wide + rows + width, wide + rows + 2 * width)
    depth, size, _ = fresh.shape
    half = mine.shape[1]
    few = terms.shape[1] // depth
    core = info[2 * tiles_max + 3]
    parity = info[2 * tiles_max + 4]
    send = jnp.where(core == 0, info[2 * tiles_max + 1], info[2 * tiles_max + 2])
    ext[0:rows, :] = job[:, inputs]
    base[...] = ALPHA * job[:, inputs].astype(F32)
    grad[...] = job[:, outer]
    acc[...] = jnp.zeros_like(acc)

    def forward(layer, carry):
        rate = rates[layer]
        start = pl.multiple_of(send * size, size)
        fresh[layer] = ext[pl.ds(start, size), :]
        ext[rows : rows + half, :] = mine[CORES * layer + parity]
        ext[rows + half : rows + 2 * half, :] = got[CORES * layer + parity]
        agg = jnp.dot(job[:, dense], ext[...], preferred_element_type=F32)
        mix = ((1.0 - ALPHA) * agg + base[...]).astype(BF16)
        mixes[layer] = mix
        weight = weight_of(core, parity, mine, got, layer)
        pre = (1.0 - rate) * mix.astype(F32) + rate * jnp.dot(
            mix, weight, preferred_element_type=F32
        )
        gate = 0.5 * jnp.tanh(0.5 * pre) + 0.5
        silu = pre * gate
        slopes[layer] = gate + silu * (1.0 - gate)
        ext[0:rows, :] = silu.astype(BF16)
        return carry

    lax.fori_loop(0, depth, forward, 0, unroll=True)

    def backward(index, carry):
        layer = depth - 1 - index
        rate = rates[layer]
        delta = (grad[...].astype(F32) * slopes[layer]).astype(BF16)
        start = pl.multiple_of(core * half, half)
        part = mixes[layer, :, pl.ds(start, half)]
        weight = weight_of(core, parity, mine, got, layer)
        dmix = (1.0 - rate) * delta.astype(F32) + rate * lax.dot_general(
            delta, weight, (((1,), (1,)), ((), ())), preferred_element_type=F32
        )
        acc[...] += dmix
        back = jnp.dot(job[:, flipped], dmix.astype(BF16), preferred_element_type=F32)
        gx = (1.0 - ALPHA) * back
        grad[...] = gx.astype(BF16)
        dweight = lax.dot_general(
            part, delta, (((0,), (0,)), ((), ())), preferred_element_type=F32
        ).astype(BF16)
        row = pl.multiple_of(layer * few, few)
        for piece in range(PARTS):
            terms[piece, pl.ds(row, few), :] = dweight[piece * few : (piece + 1) * few]

        @pl.when(layer == 0)
        def _():
            last[...] = gx

        return carry

    lax.fori_loop(0, depth, backward, 0, unroll=True)
    turned[...] = (ALPHA * acc[...] + last[...]).T.astype(BF16)
    share = width // depth
    hop = share // 2
    for part in range(depth):
        first = pl.multiple_of(part * share + core * hop, hop)
        piece = turned[pl.ds(first, hop), :]
        columns[part, :hop, :] = piece[:, :width]
        columns[part, hop:, : width // 2] = piece[:, width:]
        columns[part, hop:, width // 2 :] = jnp.zeros((hop, width // 2), BF16)


def merge_body(pieces, fresh, columns, parcel):
    depth, size, _ = fresh.shape
    few = pieces.shape[1] // depth
    middle = size + columns.shape[1]
    for layer in range(depth):
        parcel[layer, :size, :] = fresh[layer]
        parcel[layer, size:middle, :] = columns[layer]
        rows = slice(layer * few, (layer + 1) * few)
        total = pieces[0, rows, :].astype(F32)
        for chip in range(1, pieces.shape[0]):
            total += pieces[chip, rows, :].astype(F32)
        parcel[layer, middle:, :] = total.astype(BF16)


def part_body(core_ref, arrived, stays, leaves, held, handed):
    spans, size, _ = stays.shape
    spare = held.shape[1]
    core = core_ref[0]
    for span in range(spans):
        near = core * spans + span
        away = (1 - core) * spans + span
        leaves[span] = arrived[near, :size, :]
        stays[span] = arrived[away, :size, :]
        held[span] = arrived[near, size : size + spare, :]
        handed[span] = arrived[away, size : size + spare, :]


def unpack_body(core_ref, held, passed, out):
    spans, share, _ = out.shape
    width = held.shape[-1]
    hop = share // 2
    core = core_ref[0]
    for half, source in ((core, held), (1 - core, passed)):
        rows = pl.ds(pl.multiple_of(half * hop, hop), hop)
        for span in range(spans):
            out[span, rows, :width] = source[span, :hop, :].astype(F32)
            out[span, rows, width:] = source[span, hop:, : width // 2].astype(F32)


def fresh_body(core_ref, stays, comes, out):
    size = stays.shape[1]
    first = core_ref[0] == 0
    for span in range(stays.shape[0]):
        own, other = stays[span], comes[span]
        out[0, span, :size, :] = jnp.where(first, other, own)
        out[0, span, size:, :] = jnp.where(first, own, other)


def assemble_body(spread, out):
    peers, few, _ = spread.shape
    for core in range(CORES):
        for chip in range(peers // CORES):
            row = (core * (peers // CORES) + chip) * few
            out[0, row : row + few, :] = spread[CORES * chip + core].astype(F32)


def swap(value):
    size = lax.axis_size("dom")
    return lax.ppermute(value, "dom", [(i, i ^ 1) for i in range(size)])


def exchange(value, axis, groups=None):
    return lax.all_to_all(value, axis, 0, 0, tiled=True, axis_index_groups=groups)


def shards(
    initial_embed,
    out_cotangent,
    layer_weights,
    stale_halo,
    tile_values,
    tile_rows,
    tile_cols,
    tile_count,
    send_blocks,
):
    section = lax.axis_index("section")
    depth = lax.axis_size("section")
    doms = lax.axis_size("dom")
    core = lax.axis_index("dom") % CORES
    spans, rows, width = initial_embed.shape
    tiles_max, size = tile_values.shape[1], tile_values.shape[-1]
    nblocks = rows // size
    half = width // 2
    chips = doms // CORES
    span = section % spans
    parity = section // spans
    core_ref = core.astype(jnp.int32)[None]
    rates = jnp.log(LAMBDA_RATE / (jnp.arange(depth, dtype=F32) + 1.0) + 1.0)

    slots = call(
        slots_body,
        jax.ShapeDtypeStruct((CORES, spans, CORES, size, width), BF16),
        [smem(), anywhere(), anywhere()],
        [
            pltpu.VMEM((spans, CORES, size, width), BF16),
            pltpu.VMEM((CORES, half, width), BF16),
            pltpu.SemaphoreType.DMA((2,)),
            pltpu.SemaphoreType.DMA((1 + spans,)),
        ],
        10**5,
        10**6,
        anywhere,
        LARGE,
    )(
        core.astype(jnp.int32)[None],
        stale_halo.reshape(spans, CORES, size, width),
        layer_weights.reshape(CORES, half, width),
    ).reshape(depth * CORES, size, width)
    column = [
        [z * doms + CORES * i + j for z in range(depth) for j in range(CORES)] for i in range(chips)
    ]
    mine = exchange(slots, ("section", "dom"), column)

    def of_span(value):
        return lax.dynamic_index_in_dim(value, span, 0, keepdims=False)

    own_x, own_g, own_t = of_span(initial_embed), of_span(out_cotangent), of_span(tile_values)
    own_info = jnp.concatenate(
        [of_span(tile_rows), of_span(tile_cols), of_span(tile_count), of_span(send_blocks)]
    )
    is_mine = parity == core
    info = jnp.where(is_mine, own_info, swap(own_info))
    info = jnp.concatenate(
        [info, core.astype(jnp.int32)[None], parity.astype(jnp.int32)[None]]
    )
    wide = rows + 2 * size
    job = call(
        functools.partial(prepare_body, tiles_max, nblocks),
        jax.ShapeDtypeStruct((rows, wide + rows + 2 * width), BF16),
        [smem()] + [vmem()] * 6,
        [pltpu.VMEM((nblocks, nblocks + 2, size, size), F32)],
        10**6,
        4 * 10**6,
    )(info, own_x, swap(own_x), own_g, swap(own_g), own_t, swap(own_t))

    mine, job = lax.optimization_barrier((mine, job))
    got = swap(mine)

    few = half // PARTS
    spare = width // depth
    fresh_out, terms, columns = call(
        functools.partial(chain_body, tiles_max),
        (
            jax.ShapeDtypeStruct((depth, size, width), BF16),
            jax.ShapeDtypeStruct((PARTS, depth * few, width), BF16),
            jax.ShapeDtypeStruct((depth, spare, width), BF16),
        ),
        [smem()] * 2 + [vmem()] * 3,
        [
            pltpu.VMEM((rows, width), BF16),
            pltpu.VMEM((wide, width), BF16),
            pltpu.VMEM((rows, width), F32),
            pltpu.VMEM((depth, rows, width), BF16),
            pltpu.VMEM((depth, rows, width), F32),
            pltpu.VMEM((rows, width), F32),
            pltpu.VMEM((rows, width), F32),
            pltpu.VMEM((width, rows), BF16),
        ],
        2800 * 10**6,
        10**7,
    )(info, rates, job, mine, got)

    chips_y = chips // CHIPS_X
    far_y = chips_y // NEAR_Y

    def dom_of(x, far, near, j):
        return (x * chips_y + far * NEAR_Y + near) * CORES + j

    xs, nears, fars, cores = range(CHIPS_X), range(NEAR_Y), range(far_y), range(CORES)
    block = [[dom_of(x, f, n, j) for x in xs for n in nears] for f in fars for j in cores]
    along_y = [[dom_of(x, f, n, j) for f in fars] for x in xs for n in nears for j in cores]
    plane = [[dom_of(x, f, n, j) for x in xs for n in nears for j in cores] for f in fars]
    pieces = exchange(terms, "dom", block)
    parcel = call(
        merge_body,
        jax.ShapeDtypeStruct((depth, size + spare + few, width), BF16),
        [vmem()] * 3,
        [],
        10**6,
        10**6,
    )(pieces, fresh_out, columns)

    arrived = exchange(parcel, "section")
    scale = 1.0 / math.sqrt(spans * rows * doms)
    piece = arrived[:, size + spare :, :].astype(F32).sum(axis=0).astype(BF16)
    copies = jnp.broadcast_to(piece[None], (far_y,) + piece.shape)
    copies, arrived = lax.optimization_barrier((copies, arrived))
    piece = exchange(copies, "dom", along_y).astype(F32).sum(axis=0) * scale
    stays, leaves, held, handed = call(
        part_body,
        (
            jax.ShapeDtypeStruct((spans, size, width), BF16),
            jax.ShapeDtypeStruct((spans, size, width), BF16),
            jax.ShapeDtypeStruct((spans, spare, width), BF16),
            jax.ShapeDtypeStruct((spans, spare, width), BF16),
        ),
        [smem(), vmem()],
        [],
        100,
        100,
    )(core_ref, arrived)
    comes = lax.ppermute(
        leaves, "dom", [(i, (i - 1) % doms if i % 2 == 0 else (i + 1) % doms) for i in range(doms)]
    )
    fresh = call(
        fresh_body,
        jax.ShapeDtypeStruct((1, spans, 2 * size, width), BF16),
        [smem(), vmem(), vmem()],
        [],
        100,
        100,
    )(core_ref, stays, comes)
    piece = piece.astype(BF16)
    copies = jnp.broadcast_to(piece[None], (PARTS * CORES,) + piece.shape)
    copies, handed = lax.optimization_barrier((copies, handed))
    spread = exchange(copies, "dom", plane)
    weight_grad = call(
        assemble_body,
        jax.ShapeDtypeStruct((1, width, width), F32),
        [vmem()],
        [],
        100,
        100,
    )(spread)

    passed = swap(handed)
    initial_grad = call(
        unpack_body,
        jax.ShapeDtypeStruct((spans, width // depth, rows), F32),
        [smem(), vmem(), vmem()],
        [],
        100,
        100,
    )(core_ref, held, passed)
    return (weight_grad, fresh, initial_grad.transpose(0, 2, 1))


def solution(mesh):
    placed = (
        P(None, "dom", None),
        P(None, "dom", None),
        P("section", None, None),
        P("section", None, "dom", None),
        P(None, "dom", None, None),
        P(None, "dom"),
        P(None, "dom"),
        P(None, "dom"),
        P(None, "dom"),
    )
    return jax.shard_map(
        shards,
        mesh=mesh,
        in_specs=placed,
        out_specs=(
            P("section", None, None),
            P("section", None, "dom", None),
            P(None, "dom", "section"),
        ),
        check_vma=False,
    )
```

```python
import functools
import math

import jax
import jax.numpy as jnp
from jax import lax
from jax.experimental import pallas as pl
from jax.experimental.pallas import tpu as pltpu
from jax.sharding import PartitionSpec as P

ALPHA = 0.1
LAMBDA_RATE = 0.5
CORES = 2
CHIPS_X = 4
NEAR_Y = 2
PARTS = CHIPS_X * NEAR_Y
LARGE = 56
F32 = jnp.float32
BF16 = jnp.bfloat16


def vmem():
    return pl.BlockSpec(memory_space=pltpu.VMEM)


def smem():
    return pl.BlockSpec(memory_space=pltpu.SMEM)


def anywhere():
    return pl.BlockSpec(memory_space=pl.ANY)


def call(body, out_shape, in_specs, scratch, flops, moved, place=vmem, mib=24):
    return pl.pallas_call(
        body,
        out_shape=out_shape,
        in_specs=in_specs,
        out_specs=jax.tree.map(lambda _: place(), out_shape),
        scratch_shapes=scratch,
        compiler_params=pltpu.CompilerParams(vmem_limit_bytes=mib * 1024 * 1024),
        cost_estimate=pl.CostEstimate(flops=flops, bytes_accessed=moved, transcendentals=0),
    )


def slots_body(core_ref, halo_far, weight_far, out, halo, weight, fetched, sent):
    spans = halo.shape[0]
    core = core_ref[0]
    weight_in = pltpu.make_async_copy(weight_far, weight, fetched.at[0])
    halo_in = [
        pltpu.make_async_copy(halo_far.at[span], halo.at[span], fetched.at[1 + span])
        for span in range(spans)
    ]
    weight_in.start()
    for copy in halo_in:
        copy.start()
    copies = [
        pltpu.make_async_copy(weight, out.at[1 - core, span], sent.at[span])
        for span in range(spans)
    ] + [
        pltpu.make_async_copy(halo.at[span], out.at[core, span], sent.at[spans + span])
        for span in range(spans)
    ]
    weight_in.wait()
    for copy in copies[:spans]:
        copy.start()
    for span in range(spans):
        halo_in[span].wait()
        copies[spans + span].start()
    for copy in copies:
        copy.wait()


def prepare_body(
    tiles_max, nblocks, info, own_x, got_x, own_g, got_g, own_t, got_t, job, acc
):
    size = acc.shape[-1]
    core = info[2 * tiles_max + 3]
    mine = info[2 * tiles_max + 4] == core
    acc[...] = jnp.zeros_like(acc)

    def add(slot, carry):
        row = info[slot]
        col = info[tiles_max + slot]
        col = jnp.where(col < nblocks, col, nblocks + jnp.where(col - nblocks == core, 0, 1))
        tile = jnp.where(mine, own_t[slot], got_t[slot])
        acc[row, col] += tile.astype(F32)
        return carry

    lax.fori_loop(0, info[2 * tiles_max], add, 0)
    for row in range(nblocks):
        for col in range(nblocks + 2):
            block = acc[row, col]
            job[row * size : (row + 1) * size, col * size : (col + 1) * size] = block.astype(BF16)
            if col < nblocks:
                lane = (nblocks + 2 + row) * size
                job[col * size : (col + 1) * size, lane : lane + size] = block.T.astype(BF16)
    lane = (2 * nblocks + 2) * size
    width = own_x.shape[1]
    job[:, lane : lane + width] = jnp.where(mine, own_x[...], got_x[...])
    job[:, lane + width : lane + 2 * width] = jnp.where(mine, own_g[...], got_g[...])


def weight_of(core, parity, mine, got, layer):
    own = mine[CORES * layer + 1 - parity]
    other = got[CORES * layer + 1 - parity]
    top = jnp.where(core == 0, own, other)
    bottom = jnp.where(core == 0, other, own)
    return jnp.concatenate([top, bottom], axis=0)


def chain_body(
    tiles_max, info, rates, job, mine, got, fresh, terms, columns,
    grad, ext, base, mixes, slopes, acc, last, turned
):
    rows, width = base.shape
    wide = ext.shape[0]
    dense = slice(0, wide)
    flipped = slice(wide, wide + rows)
    inputs = slice(wide + rows, wide + rows + width)
    outer = slice(wide + rows + width, wide + rows + 2 * width)
    depth, size, _ = fresh.shape
    half = mine.shape[1]
    few = terms.shape[1] // depth
    core = info[2 * tiles_max + 3]
    parity = info[2 * tiles_max + 4]
    send = jnp.where(core == 0, info[2 * tiles_max + 1], info[2 * tiles_max + 2])
    ext[0:rows, :] = job[:, inputs]
    base[...] = ALPHA * job[:, inputs].astype(F32)
    grad[...] = job[:, outer]
    acc[...] = jnp.zeros_like(acc)

    def forward(layer, carry):
        rate = rates[layer]
        start = pl.multiple_of(send * size, size)
        fresh[layer] = ext[pl.ds(start, size), :]
        ext[rows : rows + half, :] = mine[CORES * layer + parity]
        ext[rows + half : rows + 2 * half, :] = got[CORES * layer + parity]
        agg = jnp.dot(job[:, dense], ext[...], preferred_element_type=F32)
        mix = ((1.0 - ALPHA) * agg + base[...]).astype(BF16)
        mixes[layer] = mix
        weight = weight_of(core, parity, mine, got, layer)
        pre = (1.0 - rate) * mix.astype(F32) + rate * jnp.dot(
            mix, weight, preferred_element_type=F32
        )
        gate = 0.5 * jnp.tanh(0.5 * pre) + 0.5
        silu = pre * gate
        slopes[layer] = gate + silu * (1.0 - gate)
        ext[0:rows, :] = silu.astype(BF16)
        return carry

    lax.fori_loop(0, depth, forward, 0, unroll=True)

    def backward(index, carry):
        layer = depth - 1 - index
        rate = rates[layer]
        delta = (grad[...].astype(F32) * slopes[layer]).astype(BF16)
        start = pl.multiple_of(core * half, half)
        part = mixes[layer, :, pl.ds(start, half)]
        weight = weight_of(core, parity, mine, got, layer)
        dmix = (1.0 - rate) * delta.astype(F32) + rate * lax.dot_general(
            delta, weight, (((1,), (1,)), ((), ())), preferred_element_type=F32
        )
        acc[...] += dmix
        back = jnp.dot(job[:, flipped], dmix.astype(BF16), preferred_element_type=F32)
        gx = (1.0 - ALPHA) * back
        grad[...] = gx.astype(BF16)
        dweight = lax.dot_general(
            part, delta, (((0,), (0,)), ((), ())), preferred_element_type=F32
        ).astype(BF16)
        row = pl.multiple_of(layer * few, few)
        for piece in range(PARTS):
            terms[piece, pl.ds(row, few), :] = dweight[piece * few : (piece + 1) * few]

        @pl.when(layer == 0)
        def _():
            last[...] = gx

        return carry

    lax.fori_loop(0, depth, backward, 0, unroll=True)
    turned[...] = (ALPHA * acc[...] + last[...]).T.astype(BF16)
    share = width // depth
    hop = share // 2
    for part in range(depth):
        first = pl.multiple_of(part * share + core * hop, hop)
        piece = turned[pl.ds(first, hop), :]
        columns[part, :hop, :] = piece[:, :width]
        columns[part, hop:, : width // 2] = piece[:, width:]
        columns[part, hop:, width // 2 :] = jnp.zeros((hop, width // 2), BF16)


def merge_body(pieces, fresh, columns, parcel):
    depth, size, _ = fresh.shape
    few = pieces.shape[1] // depth
    middle = size + columns.shape[1]
    for layer in range(depth):
        parcel[layer, :size, :] = fresh[layer]
        parcel[layer, size:middle, :] = columns[layer]
        rows = slice(layer * few, (layer + 1) * few)
        total = pieces[0, rows, :].astype(F32)
        for chip in range(1, pieces.shape[0]):
            total += pieces[chip, rows, :].astype(F32)
        parcel[layer, middle:, :] = total.astype(BF16)


def part_body(core_ref, arrived, stays, leaves, held, handed):
    spans, size, _ = stays.shape
    spare = held.shape[1]
    core = core_ref[0]
    for span in range(spans):
        near = core * spans + span
        away = (1 - core) * spans + span
        leaves[span] = arrived[near, :size, :]
        stays[span] = arrived[away, :size, :]
        held[span] = arrived[near, size : size + spare, :]
        handed[span] = arrived[away, size : size + spare, :]


def finish_body(core_ref, held, passed, stays, comes, out, fresh):
    fresh_body(core_ref, stays, comes, fresh)
    spans, share, _ = out.shape
    width = held.shape[-1]
    hop = share // 2
    core = core_ref[0]
    for half, source in ((core, held), (1 - core, passed)):
        rows = pl.ds(pl.multiple_of(half * hop, hop), hop)
        for span in range(spans):
            out[span, rows, :width] = source[span, :hop, :].astype(F32)
            out[span, rows, width:] = source[span, hop:, : width // 2].astype(F32)


def fresh_body(core_ref, stays, comes, out):
    size = stays.shape[1]
    first = core_ref[0] == 0
    for span in range(stays.shape[0]):
        own, other = stays[span], comes[span]
        out[0, span, :size, :] = jnp.where(first, other, own)
        out[0, span, size:, :] = jnp.where(first, own, other)


def assemble_body(spread, out):
    peers, few, _ = spread.shape
    for core in range(CORES):
        for chip in range(peers // CORES):
            row = (core * (peers // CORES) + chip) * few
            out[0, row : row + few, :] = spread[CORES * chip + core].astype(F32)


def swap(value):
    size = lax.axis_size("dom")
    return lax.ppermute(value, "dom", [(i, i ^ 1) for i in range(size)])


def exchange(value, axis, groups=None):
    return lax.all_to_all(value, axis, 0, 0, tiled=True, axis_index_groups=groups)


def shards(
    initial_embed,
    out_cotangent,
    layer_weights,
    stale_halo,
    tile_values,
    tile_rows,
    tile_cols,
    tile_count,
    send_blocks,
):
    section = lax.axis_index("section")
    depth = lax.axis_size("section")
    doms = lax.axis_size("dom")
    core = lax.axis_index("dom") % CORES
    spans, rows, width = initial_embed.shape
    tiles_max, size = tile_values.shape[1], tile_values.shape[-1]
    nblocks = rows // size
    half = width // 2
    chips = doms // CORES
    span = section % spans
    parity = section // spans
    core_ref = core.astype(jnp.int32)[None]
    rates = jnp.log(LAMBDA_RATE / (jnp.arange(depth, dtype=F32) + 1.0) + 1.0)

    slots = call(
        slots_body,
        jax.ShapeDtypeStruct((CORES, spans, CORES, size, width), BF16),
        [smem(), anywhere(), anywhere()],
        [
            pltpu.VMEM((spans, CORES, size, width), BF16),
            pltpu.VMEM((CORES, half, width), BF16),
            pltpu.SemaphoreType.DMA((1 + spans,)),
            pltpu.SemaphoreType.DMA((2 * spans,)),
        ],
        10**5,
        10**6,
        anywhere,
        LARGE,
    )(
        core.astype(jnp.int32)[None],
        stale_halo.reshape(spans, CORES, size, width),
        layer_weights.reshape(CORES, half, width),
    ).reshape(depth * CORES, size, width)
    column = [
        [z * doms + CORES * i + j for z in range(depth) for j in range(CORES)] for i in range(chips)
    ]
    mine = exchange(slots, ("section", "dom"), column)

    def of_span(value):
        return lax.dynamic_index_in_dim(value, span, 0, keepdims=False)

    own_x, own_g, own_t = of_span(initial_embed), of_span(out_cotangent), of_span(tile_values)
    own_info = jnp.concatenate(
        [of_span(tile_rows), of_span(tile_cols), of_span(tile_count), of_span(send_blocks)]
    )
    is_mine = parity == core
    info = jnp.where(is_mine, own_info, swap(own_info))
    info = jnp.concatenate(
        [info, core.astype(jnp.int32)[None], parity.astype(jnp.int32)[None]]
    )
    wide = rows + 2 * size
    job = call(
        functools.partial(prepare_body, tiles_max, nblocks),
        jax.ShapeDtypeStruct((rows, wide + rows + 2 * width), BF16),
        [smem()] + [vmem()] * 6,
        [pltpu.VMEM((nblocks, nblocks + 2, size, size), F32)],
        10**6,
        4 * 10**6,
    )(info, own_x, swap(own_x), own_g, swap(own_g), own_t, swap(own_t))

    mine, job = lax.optimization_barrier((mine, job))
    got = swap(mine)

    few = half // PARTS
    spare = width // depth
    fresh_out, terms, columns = call(
        functools.partial(chain_body, tiles_max),
        (
            jax.ShapeDtypeStruct((depth, size, width), BF16),
            jax.ShapeDtypeStruct((PARTS, depth * few, width), BF16),
            jax.ShapeDtypeStruct((depth, spare, width), BF16),
        ),
        [smem()] * 2 + [vmem()] * 3,
        [
            pltpu.VMEM((rows, width), BF16),
            pltpu.VMEM((wide, width), BF16),
            pltpu.VMEM((rows, width), F32),
            pltpu.VMEM((depth, rows, width), BF16),
            pltpu.VMEM((depth, rows, width), F32),
            pltpu.VMEM((rows, width), F32),
            pltpu.VMEM((rows, width), F32),
            pltpu.VMEM((width, rows), BF16),
        ],
        2800 * 10**6,
        10**7,
    )(info, rates, job, mine, got)

    chips_y = chips // CHIPS_X
    far_y = chips_y // NEAR_Y

    def dom_of(x, far, near, j):
        return (x * chips_y + far * NEAR_Y + near) * CORES + j

    xs, nears, fars, cores = range(CHIPS_X), range(NEAR_Y), range(far_y), range(CORES)
    block = [[dom_of(x, f, n, j) for x in xs for n in nears] for f in fars for j in cores]
    along_y = [[dom_of(x, f, n, j) for f in fars] for x in xs for n in nears for j in cores]
    plane = [[dom_of(x, f, n, j) for x in xs for n in nears for j in cores] for f in fars]
    pieces = exchange(terms, "dom", block)
    parcel = call(
        merge_body,
        jax.ShapeDtypeStruct((depth, size + spare + few, width), BF16),
        [vmem()] * 3,
        [],
        10**6,
        10**6,
    )(pieces, fresh_out, columns)

    arrived = exchange(parcel, "section")
    scale = 1.0 / math.sqrt(spans * rows * doms)
    piece = arrived[:, size + spare :, :].astype(F32).sum(axis=0).astype(BF16)
    copies = jnp.broadcast_to(piece[None], (far_y,) + piece.shape)
    copies, arrived = lax.optimization_barrier((copies, arrived))
    piece = exchange(copies, "dom", along_y).astype(F32).sum(axis=0) * scale
    stays, leaves, held, handed = call(
        part_body,
        (
            jax.ShapeDtypeStruct((spans, size, width), BF16),
            jax.ShapeDtypeStruct((spans, size, width), BF16),
            jax.ShapeDtypeStruct((spans, spare, width), BF16),
            jax.ShapeDtypeStruct((spans, spare, width), BF16),
        ),
        [smem(), vmem()],
        [],
        100,
        100,
    )(core_ref, arrived)
    comes = lax.ppermute(
        leaves, "dom", [(i, (i - 1) % doms if i % 2 == 0 else (i + 1) % doms) for i in range(doms)]
    )
    piece = piece.astype(BF16)
    copies = jnp.broadcast_to(piece[None], (PARTS * CORES,) + piece.shape)
    copies, handed = lax.optimization_barrier((copies, handed))
    spread = exchange(copies, "dom", plane)
    weight_grad = call(
        assemble_body,
        jax.ShapeDtypeStruct((1, width, width), F32),
        [vmem()],
        [],
        100,
        100,
    )(spread)

    passed = swap(handed)
    initial_grad, fresh = call(
        finish_body,
        (
            jax.ShapeDtypeStruct((spans, width // depth, rows), F32),
            jax.ShapeDtypeStruct((1, spans, 2 * size, width), BF16),
        ),
        [smem()] + [vmem()] * 4,
        [],
        100,
        100,
    )(core_ref, held, passed, stays, comes)
    return (weight_grad, fresh, initial_grad.transpose(0, 2, 1))


def solution(mesh):
    placed = (
        P(None, "dom", None),
        P(None, "dom", None),
        P("section", None, None),
        P("section", None, "dom", None),
        P(None, "dom", None, None),
        P(None, "dom"),
        P(None, "dom"),
        P(None, "dom"),
        P(None, "dom"),
    )
    return jax.shard_map(
        shards,
        mesh=mesh,
        in_specs=placed,
        out_specs=(
            P("section", None, None),
            P("section", None, "dom", None),
            P(None, "dom", "section"),
        ),
        check_vma=False,
    )
```

```python
import functools
import math

import jax
import jax.numpy as jnp
from jax import lax
from jax.experimental import pallas as pl
from jax.experimental.pallas import tpu as pltpu
from jax.sharding import PartitionSpec as P

ALPHA = 0.1
LAMBDA_RATE = 0.5
CORES = 2
CHIPS_X = 4
NEAR_Y = 2
PARTS = CHIPS_X * NEAR_Y
LARGE = 56
F32 = jnp.float32
BF16 = jnp.bfloat16


def vmem():
    return pl.BlockSpec(memory_space=pltpu.VMEM)


def smem():
    return pl.BlockSpec(memory_space=pltpu.SMEM)


def anywhere():
    return pl.BlockSpec(memory_space=pl.ANY)


def call(body, out_shape, in_specs, scratch, flops, moved, place=vmem, mib=24):
    return pl.pallas_call(
        body,
        out_shape=out_shape,
        in_specs=in_specs,
        out_specs=jax.tree.map(lambda _: place(), out_shape),
        scratch_shapes=scratch,
        compiler_params=pltpu.CompilerParams(vmem_limit_bytes=mib * 1024 * 1024),
        cost_estimate=pl.CostEstimate(flops=flops, bytes_accessed=moved, transcendentals=0),
    )


def slots_body(core_ref, halo_far, weight_far, out, halo, weight, fetched, sent):
    spans = halo.shape[0]
    core = core_ref[0]
    weight_in = pltpu.make_async_copy(weight_far, weight, fetched.at[0])
    halo_in = [
        pltpu.make_async_copy(halo_far.at[span], halo.at[span], fetched.at[1 + span])
        for span in range(spans)
    ]
    weight_in.start()
    for copy in halo_in:
        copy.start()
    copies = [
        pltpu.make_async_copy(weight, out.at[1 - core, span], sent.at[span])
        for span in range(spans)
    ] + [
        pltpu.make_async_copy(halo.at[span], out.at[core, span], sent.at[spans + span])
        for span in range(spans)
    ]
    weight_in.wait()
    for copy in copies[:spans]:
        copy.start()
    for span in range(spans):
        halo_in[span].wait()
        copies[spans + span].start()
    for copy in copies:
        copy.wait()


def prepare_body(
    tiles_max, nblocks, info, own_x, got_x, own_g, got_g, own_t, got_t, job, acc
):
    size = acc.shape[-1]
    core = info[2 * tiles_max + 3]
    mine = info[2 * tiles_max + 4] == core
    acc[...] = jnp.zeros_like(acc)

    def add(slot, carry):
        row = info[slot]
        col = info[tiles_max + slot]
        col = jnp.where(col < nblocks, col, nblocks + jnp.where(col - nblocks == core, 0, 1))
        tile = jnp.where(mine, own_t[slot], got_t[slot])
        acc[row, col] += tile.astype(F32)
        return carry

    lax.fori_loop(0, info[2 * tiles_max], add, 0)
    for row in range(nblocks):
        for col in range(nblocks + 2):
            block = acc[row, col]
            job[row * size : (row + 1) * size, col * size : (col + 1) * size] = block.astype(BF16)
            if col < nblocks:
                lane = (nblocks + 2 + row) * size
                job[col * size : (col + 1) * size, lane : lane + size] = block.T.astype(BF16)
    lane = (2 * nblocks + 2) * size
    width = own_x.shape[1]
    job[:, lane : lane + width] = jnp.where(mine, own_x[...], got_x[...])
    job[:, lane + width : lane + 2 * width] = jnp.where(mine, own_g[...], got_g[...])


def weight_of(core, parity, mine, got, layer):
    own = mine[CORES * layer + 1 - parity]
    other = got[CORES * layer + 1 - parity]
    top = jnp.where(core == 0, own, other)
    bottom = jnp.where(core == 0, other, own)
    return jnp.concatenate([top, bottom], axis=0)


def chain_body(
    tiles_max, info, rates, job, mine_far, got, fresh, terms, columns,
    grad, ext, base, mixes, slopes, acc, last, turned, mine, fetched
):
    fetch = pltpu.make_async_copy(mine_far, mine, fetched.at[0])
    fetch.start()
    rows, width = base.shape
    wide = ext.shape[0]
    dense = slice(0, wide)
    flipped = slice(wide, wide + rows)
    inputs = slice(wide + rows, wide + rows + width)
    outer = slice(wide + rows + width, wide + rows + 2 * width)
    depth, size, _ = fresh.shape
    half = mine.shape[1]
    few = terms.shape[1] // depth
    core = info[2 * tiles_max + 3]
    parity = info[2 * tiles_max + 4]
    send = jnp.where(core == 0, info[2 * tiles_max + 1], info[2 * tiles_max + 2])
    ext[0:rows, :] = job[:, inputs]
    base[...] = ALPHA * job[:, inputs].astype(F32)
    grad[...] = job[:, outer]
    acc[...] = jnp.zeros_like(acc)
    fetch.wait()

    def forward(layer, carry):
        rate = rates[layer]
        start = pl.multiple_of(send * size, size)
        fresh[layer] = ext[pl.ds(start, size), :]
        ext[rows : rows + half, :] = mine[CORES * layer + parity]
        ext[rows + half : rows + 2 * half, :] = got[CORES * layer + parity]
        agg = jnp.dot(job[:, dense], ext[...], preferred_element_type=F32)
        mix = ((1.0 - ALPHA) * agg + base[...]).astype(BF16)
        mixes[layer] = mix
        weight = weight_of(core, parity, mine, got, layer)
        pre = (1.0 - rate) * mix.astype(F32) + rate * jnp.dot(
            mix, weight, preferred_element_type=F32
        )
        gate = 0.5 * jnp.tanh(0.5 * pre) + 0.5
        silu = pre * gate
        slopes[layer] = gate + silu * (1.0 - gate)
        ext[0:rows, :] = silu.astype(BF16)
        return carry

    lax.fori_loop(0, depth, forward, 0, unroll=True)

    def backward(index, carry):
        layer = depth - 1 - index
        rate = rates[layer]
        delta = (grad[...].astype(F32) * slopes[layer]).astype(BF16)
        start = pl.multiple_of(core * half, half)
        part = mixes[layer, :, pl.ds(start, half)]
        weight = weight_of(core, parity, mine, got, layer)
        dmix = (1.0 - rate) * delta.astype(F32) + rate * lax.dot_general(
            delta, weight, (((1,), (1,)), ((), ())), preferred_element_type=F32
        )
        acc[...] += dmix
        back = jnp.dot(job[:, flipped], dmix.astype(BF16), preferred_element_type=F32)
        gx = (1.0 - ALPHA) * back
        grad[...] = gx.astype(BF16)
        dweight = lax.dot_general(
            part, delta, (((0,), (0,)), ((), ())), preferred_element_type=F32
        ).astype(BF16)
        row = pl.multiple_of(layer * few, few)
        for piece in range(PARTS):
            terms[piece, pl.ds(row, few), :] = dweight[piece * few : (piece + 1) * few]

        @pl.when(layer == 0)
        def _():
            last[...] = gx

        return carry

    lax.fori_loop(0, depth, backward, 0, unroll=True)
    turned[...] = (ALPHA * acc[...] + last[...]).T.astype(BF16)
    share = width // depth
    hop = share // 2
    for part in range(depth):
        first = pl.multiple_of(part * share + core * hop, hop)
        piece = turned[pl.ds(first, hop), :]
        columns[part, :hop, :] = piece[:, :width]
        columns[part, hop:, : width // 2] = piece[:, width:]
        columns[part, hop:, width // 2 :] = jnp.zeros((hop, width // 2), BF16)


def merge_body(pieces, fresh, columns, parcel):
    depth, size, _ = fresh.shape
    few = pieces.shape[1] // depth
    middle = size + columns.shape[1]
    for layer in range(depth):
        parcel[layer, :size, :] = fresh[layer]
        parcel[layer, size:middle, :] = columns[layer]
        rows = slice(layer * few, (layer + 1) * few)
        total = pieces[0, rows, :].astype(F32)
        for chip in range(1, pieces.shape[0]):
            total += pieces[chip, rows, :].astype(F32)
        parcel[layer, middle:, :] = total.astype(BF16)


def part_body(core_ref, arrived, stays, leaves, held, handed):
    spans, size, _ = stays.shape
    spare = held.shape[1]
    core = core_ref[0]
    for span in range(spans):
        near = core * spans + span
        away = (1 - core) * spans + span
        leaves[span] = arrived[near, :size, :]
        stays[span] = arrived[away, :size, :]
        held[span] = arrived[near, size : size + spare, :]
        handed[span] = arrived[away, size : size + spare, :]


def finish_body(core_ref, held, passed, stays, comes, out, fresh):
    fresh_body(core_ref, stays, comes, fresh)
    spans, share, _ = out.shape
    width = held.shape[-1]
    hop = share // 2
    core = core_ref[0]
    for half, source in ((core, held), (1 - core, passed)):
        rows = pl.ds(pl.multiple_of(half * hop, hop), hop)
        for span in range(spans):
            out[span, rows, :width] = source[span, :hop, :].astype(F32)
            out[span, rows, width:] = source[span, hop:, : width // 2].astype(F32)


def fresh_body(core_ref, stays, comes, out):
    size = stays.shape[1]
    first = core_ref[0] == 0
    for span in range(stays.shape[0]):
        own, other = stays[span], comes[span]
        out[0, span, :size, :] = jnp.where(first, other, own)
        out[0, span, size:, :] = jnp.where(first, own, other)


def assemble_body(spread, out):
    peers, few, _ = spread.shape
    for core in range(CORES):
        for chip in range(peers // CORES):
            row = (core * (peers // CORES) + chip) * few
            out[0, row : row + few, :] = spread[CORES * chip + core].astype(F32)


def swap(value):
    size = lax.axis_size("dom")
    return lax.ppermute(value, "dom", [(i, i ^ 1) for i in range(size)])


def exchange(value, axis, groups=None):
    return lax.all_to_all(value, axis, 0, 0, tiled=True, axis_index_groups=groups)


def shards(
    initial_embed,
    out_cotangent,
    layer_weights,
    stale_halo,
    tile_values,
    tile_rows,
    tile_cols,
    tile_count,
    send_blocks,
):
    section = lax.axis_index("section")
    depth = lax.axis_size("section")
    doms = lax.axis_size("dom")
    core = lax.axis_index("dom") % CORES
    spans, rows, width = initial_embed.shape
    tiles_max, size = tile_values.shape[1], tile_values.shape[-1]
    nblocks = rows // size
    half = width // 2
    chips = doms // CORES
    span = section % spans
    parity = section // spans
    core_ref = core.astype(jnp.int32)[None]
    rates = jnp.log(LAMBDA_RATE / (jnp.arange(depth, dtype=F32) + 1.0) + 1.0)

    slots = call(
        slots_body,
        jax.ShapeDtypeStruct((CORES, spans, CORES, size, width), BF16),
        [smem(), anywhere(), anywhere()],
        [
            pltpu.VMEM((spans, CORES, size, width), BF16),
            pltpu.VMEM((CORES, half, width), BF16),
            pltpu.SemaphoreType.DMA((1 + spans,)),
            pltpu.SemaphoreType.DMA((2 * spans,)),
        ],
        10**5,
        10**6,
        anywhere,
        LARGE,
    )(
        core.astype(jnp.int32)[None],
        stale_halo.reshape(spans, CORES, size, width),
        layer_weights.reshape(CORES, half, width),
    ).reshape(depth * CORES, size, width)
    column = [
        [z * doms + CORES * i + j for z in range(depth) for j in range(CORES)] for i in range(chips)
    ]
    mine = exchange(slots, ("section", "dom"), column)

    def of_span(value):
        return lax.dynamic_index_in_dim(value, span, 0, keepdims=False)

    own_x, own_g, own_t = of_span(initial_embed), of_span(out_cotangent), of_span(tile_values)
    own_info = jnp.concatenate(
        [of_span(tile_rows), of_span(tile_cols), of_span(tile_count), of_span(send_blocks)]
    )
    is_mine = parity == core
    info = jnp.where(is_mine, own_info, swap(own_info))
    info = jnp.concatenate(
        [info, core.astype(jnp.int32)[None], parity.astype(jnp.int32)[None]]
    )
    wide = rows + 2 * size
    job = call(
        functools.partial(prepare_body, tiles_max, nblocks),
        jax.ShapeDtypeStruct((rows, wide + rows + 2 * width), BF16),
        [smem()] + [vmem()] * 6,
        [pltpu.VMEM((nblocks, nblocks + 2, size, size), F32)],
        10**6,
        4 * 10**6,
    )(info, own_x, swap(own_x), own_g, swap(own_g), own_t, swap(own_t))

    mine, job = lax.optimization_barrier((mine, job))
    got = swap(mine)

    few = half // PARTS
    spare = width // depth
    fresh_out, terms, columns = call(
        functools.partial(chain_body, tiles_max),
        (
            jax.ShapeDtypeStruct((depth, size, width), BF16),
            jax.ShapeDtypeStruct((PARTS, depth * few, width), BF16),
            jax.ShapeDtypeStruct((depth, spare, width), BF16),
        ),
        [smem()] * 2 + [vmem(), anywhere(), vmem()],
        [
            pltpu.VMEM((rows, width), BF16),
            pltpu.VMEM((wide, width), BF16),
            pltpu.VMEM((rows, width), F32),
            pltpu.VMEM((depth, rows, width), BF16),
            pltpu.VMEM((depth, rows, width), F32),
            pltpu.VMEM((rows, width), F32),
            pltpu.VMEM((rows, width), F32),
            pltpu.VMEM((width, rows), BF16),
            pltpu.VMEM(mine.shape, BF16),
            pltpu.SemaphoreType.DMA((1,)),
        ],
        2800 * 10**6,
        10**7,
    )(info, rates, job, mine, got)

    chips_y = chips // CHIPS_X
    far_y = chips_y // NEAR_Y

    def dom_of(x, far, near, j):
        return (x * chips_y + far * NEAR_Y + near) * CORES + j

    xs, nears, fars, cores = range(CHIPS_X), range(NEAR_Y), range(far_y), range(CORES)
    block = [[dom_of(x, f, n, j) for x in xs for n in nears] for f in fars for j in cores]
    along_y = [[dom_of(x, f, n, j) for f in fars] for x in xs for n in nears for j in cores]
    plane = [[dom_of(x, f, n, j) for x in xs for n in nears for j in cores] for f in fars]
    pieces = exchange(terms, "dom", block)
    parcel = call(
        merge_body,
        jax.ShapeDtypeStruct((depth, size + spare + few, width), BF16),
        [vmem()] * 3,
        [],
        10**6,
        10**6,
    )(pieces, fresh_out, columns)

    arrived = exchange(parcel, "section")
    scale = 1.0 / math.sqrt(spans * rows * doms)
    piece = arrived[:, size + spare :, :].astype(F32).sum(axis=0).astype(BF16)
    copies = jnp.broadcast_to(piece[None], (far_y,) + piece.shape)
    copies, arrived = lax.optimization_barrier((copies, arrived))
    piece = exchange(copies, "dom", along_y).astype(F32).sum(axis=0) * scale
    stays, leaves, held, handed = call(
        part_body,
        (
            jax.ShapeDtypeStruct((spans, size, width), BF16),
            jax.ShapeDtypeStruct((spans, size, width), BF16),
            jax.ShapeDtypeStruct((spans, spare, width), BF16),
            jax.ShapeDtypeStruct((spans, spare, width), BF16),
        ),
        [smem(), vmem()],
        [],
        100,
        100,
    )(core_ref, arrived)
    comes = lax.ppermute(
        leaves, "dom", [(i, (i - 1) % doms if i % 2 == 0 else (i + 1) % doms) for i in range(doms)]
    )
    piece = piece.astype(BF16)
    copies = jnp.broadcast_to(piece[None], (PARTS * CORES,) + piece.shape)
    copies, handed = lax.optimization_barrier((copies, handed))
    spread = exchange(copies, "dom", plane)
    weight_grad = call(
        assemble_body,
        jax.ShapeDtypeStruct((1, width, width), F32),
        [vmem()],
        [],
        100,
        100,
    )(spread)

    passed = swap(handed)
    initial_grad, fresh = call(
        finish_body,
        (
            jax.ShapeDtypeStruct((spans, width // depth, rows), F32),
            jax.ShapeDtypeStruct((1, spans, 2 * size, width), BF16),
        ),
        [smem()] + [vmem()] * 4,
        [],
        100,
        100,
    )(core_ref, held, passed, stays, comes)
    return (weight_grad, fresh, initial_grad.transpose(0, 2, 1))


def solution(mesh):
    placed = (
        P(None, "dom", None),
        P(None, "dom", None),
        P("section", None, None),
        P("section", None, "dom", None),
        P(None, "dom", None, None),
        P(None, "dom"),
        P(None, "dom"),
        P(None, "dom"),
        P(None, "dom"),
    )
    return jax.shard_map(
        shards,
        mesh=mesh,
        in_specs=placed,
        out_specs=(
            P("section", None, None),
            P("section", None, "dom", None),
            P(None, "dom", "section"),
        ),
        check_vma=False,
    )
```
